32 devices in a mesh: dp: 8 (over y, x, core), tensor: 4 (over z).
Axes of the slice: x: 2, y: 2, z: 4, core: 2. Of those that a mesh axis runs over, the one named last changes fastest.
Arguments:
- tokens: bfloat16 [8192, 1152], P(('dp', 'tensor')), may hold values from -6 to 6
- w_qkv: bfloat16 [1152, 3, 1152], P(None, None, 'tensor'), may hold values from -0.1875 to 0.1875
- w_out: bfloat16 [1152, 1152], P('tensor'), may hold values from -1.5 to 1.5
- w_fc1: bfloat16 [1152, 4608], P(None, 'tensor'), may hold values from -0.1875 to 0.1875
- b_fc1: bfloat16 [4608], P('tensor'), may hold values from -3 to 3
- w_fc2: bfloat16 [4608, 1152], P('tensor'), may hold values from -0.1875 to 0.1875
- null_embed: float32 [6, 1152], replicated, may hold values from -3 to 3
- ada_embed: float32 [8, 4, 6, 1152], P('dp'), may hold values from -4 to 4
- item_len: int32 [8, 4], P('dp'), may hold values from 0 to 1024, as said below
- null_flag: int32 [8, 4], P('dp'), may hold values 0 or 1
- head_mask: int32 [8, 4, 16], P('dp'), may hold values 0 or 1
- group_mask: int32 [8, 4, 16], P('dp'), may hold values 0 or 1
- token_keep: int32 [8192], P(('dp', 'tensor')), may hold values 0 or 1
- router_logit: float32 [8192], P(('dp', 'tensor')), may hold values from -5 to 5
- cotangent: bfloat16 [8192, 1152], P(('dp', 'tensor')), may hold values from -6 to 6
Outputs:
- output: bfloat16 [8192, 1152], P(('dp', 'tensor'))
- grad_tokens: bfloat16 [8192, 1152], P(('dp', 'tensor'))
- grad_qkv: float32 [1152, 3, 1152], P('dp', None, 'tensor')
- grad_wout: float32 [1152, 1152], P('tensor', 'dp')
- grad_fc1: float32 [1152, 4608], P('dp', 'tensor')
- grad_b1: float32 [4608], replicated
- grad_fc2: float32 [4608, 1152], P('tensor', 'dp')
- grad_null: float32 [6, 1152], replicated
The draws below stay inside these ranges and needn't reach their ends.
Inputs may be any that keep to these rules, and one draw needn't show every extreme that they name: `item_len`: each row lists a group's items: items of 1024 tokens first, then items of 256 tokens, then zeros. A row sums to at most 1024 and at least half of it, and some row sums to exactly 1024; the positions after a row's sum are padding.
All inputs are finite; a program needn't handle non-finite values. No bound on the sum of `null_flag` or of `head_mask` or of `group_mask` or of `token_keep` on one device may be relied on, other than what follows from the above.
Results may differ from the reference program's by a relative error of at most 0.015.
The reference program's roundings to bfloat16 on the way count: a program that leaves them out, or rounds other values in their place, can miss the bound.
Values may be sent and summed in bfloat16 or wider, within the bound.
No kernel may reach another device: no remote copies, remote signals or barrier semaphores. Data moves between devices by JAX's collectives and lax.ppermute only.
A program may use at most 128 MiB of HBM per device.

```python
from functools import partial
import jax
import jax.numpy as jnp
from jax import lax

D = 1152
H = 16
HD = 72
FF = 4608
CG = 16
SHORT = 256
G_TOK = 1024
GROUPS = 8
TOKENS = 8192
LONG_LEN = 1024
SLOTS = 4


def draw_item_len(key, part):
    key = jax.random.fold_in(key, 17)
    key_long, key_drop, key_full = jax.random.split(key, 3)
    long_most = G_TOK // LONG_LEN
    long_count = jax.random.randint(key_long, (GROUPS,), 0, long_most + 1)
    full_group = jax.random.randint(key_full, (), 0, GROUPS)
    is_full = jnp.arange(GROUPS) == full_group
    long_count = jnp.where(is_full, jnp.maximum(long_count, 1), long_count)
    room_left = (G_TOK - long_count * LONG_LEN) // SHORT
    drop_draw = jax.random.randint(key_drop, (GROUPS,), 0, 1 << 20)
    dropped = drop_draw % (room_left // 2 + 1)
    dropped = jnp.where(is_full, 0, dropped)
    short_count = room_left - dropped
    slot_ids = jnp.arange(SLOTS)[None, :]
    lengths = jnp.where(slot_ids < long_count[:, None], LONG_LEN, jnp.where(slot_ids < (long_count + short_count)[:, None], SHORT, 0))
    return lengths.astype(jnp.int32)


def with_ends(array, own_key, least, top_value):
    longest = array.shape.index(max(array.shape))
    spots = []
    for shift in (0, 1):
        where = [jax.random.randint(jax.random.fold_in(own_key, axis), (), 0, length) for axis, length in enumerate(array.shape)]
        where[longest] = (where[longest] + shift) % array.shape[longest]
        spots.append(tuple(where))
    return array.at[spots[0]].set(least).at[spots[1]].set(top_value)


def block_levels(key, extent, shards, low, high):
    level = 1.0
    for axis_at, blocks in shards:
        heights = jax.random.uniform(jax.random.fold_in(jax.random.fold_in(key, 6), axis_at), (blocks,), jnp.float32, low / len(shards), high / len(shards))
        level = level * jnp.repeat(jnp.exp(heights), extent[axis_at] // blocks).reshape((-1,) + (1,) * (len(extent) - 1 - axis_at))
    return level


def normal_values(key, dims, deviation, limit, shards=(), kind=jnp.bfloat16):
    values = jax.random.normal(key, dims, jnp.float32) * deviation
    if len(shards) > 0:
        values = block_levels(key, dims, shards, -0.22, 0.18) * values
    return jnp.clip(values, min=-limit, max=limit).astype(kind)


def setup_inputs(seed: int = 0) -> dict:
    splits = jax.random.split(jax.random.key(seed), 16)
    return {
        "tokens": normal_values(splits[0], (TOKENS, D), 1.0, 6.0, ((0, 32),)),
        "w_qkv": normal_values(splits[1], (D, 3, D), D ** -0.5, 0.1875, ((2, 4),)),
        "w_out": normal_values(splits[2], (D, D), (D // 64) ** -0.5, 1.5, ((0, 4),)),
        "w_fc1": normal_values(splits[3], (D, FF), D ** -0.5, 0.1875, ((1, 4),)),
        "b_fc1": normal_values(splits[4], (FF,), 0.5, 3.0, ((0, 4),)),
        "w_fc2": normal_values(splits[5], (FF, D), (FF // 4) ** -0.5, 0.1875, ((0, 4),)),
        "null_embed": normal_values(splits[6], (6, D), 0.5, 3.0, (), jnp.float32),
        "ada_embed": normal_values(splits[7], (GROUPS, SLOTS, 6, D), 0.7, 4.0, ((0, 8),), jnp.float32),
        "item_len": draw_item_len(jax.random.fold_in(splits[15], 71), 0),
        "null_flag": with_ends((jax.random.randint(splits[9], (GROUPS, SLOTS), 0, 4) < 1).astype(jnp.int32), jax.random.fold_in(splits[9], 1), 0, 1),
        "head_mask": with_ends((jax.random.randint(splits[10], (GROUPS, SLOTS, H), 0, 4) < 3).astype(jnp.int32), jax.random.fold_in(splits[10], 1), 0, 1),
        "group_mask": with_ends((jax.random.randint(splits[11], (GROUPS, SLOTS, CG), 0, 4) < 3).astype(jnp.int32), jax.random.fold_in(splits[11], 1), 0, 1),
        "token_keep": with_ends((jax.random.randint(splits[12], (TOKENS,), 0, 4) < 3).astype(jnp.int32), jax.random.fold_in(splits[12], 1), 0, 1),
        "router_logit": normal_values(splits[13], (TOKENS,), 1.0, 5.0, ((0, 32),), jnp.float32),
        "cotangent": normal_values(splits[14], (TOKENS, D), 1.0, 6.0, ((0, 32),)),
    }


EPSILON = 1e-06

@jax.custom_vjp
def low(v):
    return lax.optimization_barrier(v.astype(jnp.bfloat16)).astype(jnp.float32)

@jax.custom_vjp
def low_back(v):
    return v

def low_keep(v):
    return (low(v), None)

def low_pass(kept, grad):
    return (grad,)

def back_keep(v):
    return (v, None)

def back_low(kept, grad):
    return (low(grad),)
low.defvjp(low_keep, low_pass)
low_back.defvjp(back_keep, back_low)

def layer_norm(value):
    center = value - lax.optimization_barrier(jnp.mean(value, axis=-1, keepdims=True))
    variance = lax.optimization_barrier(jnp.mean(center * center, axis=-1, keepdims=True))
    return center * lax.rsqrt(variance + EPSILON)

def group_forward(weights, pieces):
    w_qkv, w_out, w_fc1, b_fc1, w_fc2, null_embed = weights
    x_rows, lengths, null_flags, heads_on, groups_on, keep_mask, logits, embedding = pieces
    scaling = HD ** (-0.5)
    item_ends = jnp.cumsum(lengths)
    positions = jnp.arange(G_TOK, dtype=jnp.int32)
    segment = lax.optimization_barrier(jnp.sum((item_ends[None, :] <= positions[:, None]).astype(jnp.int32), axis=1))
    one_hot = (segment[:, None] == jnp.arange(SLOTS, dtype=jnp.int32)[None, :]).astype(jnp.float32)
    modulation = embedding + null_flags.astype(jnp.float32)[:, None, None] * null_embed[None]
    per_token = jnp.dot(one_hot, modulation.reshape(SLOTS, 6 * D), precision=lax.Precision.HIGHEST).reshape(G_TOK, 6, D)
    shift_a, scale_a, gate_a, shift_m, scale_m, gate_m = [per_token[:, column] for column in range(6)]
    input_a = low(layer_norm(x_rows) * (1.0 + scale_a) + shift_a)
    qkv = low(low_back(jnp.dot(input_a, w_qkv.reshape(D, 3 * D), precision=lax.Precision.HIGHEST)))
    qkv = qkv.reshape(G_TOK, 3, H, HD).transpose(1, 2, 0, 3)
    same_doc = segment[:, None] == segment[None, :]

    def head_attend(triple):
        queries, key_rows, values = triple
        scores = low_back(jnp.dot(queries, key_rows.T, precision=lax.Precision.HIGHEST) * scaling)
        attn_prob = jax.nn.softmax(jnp.where(same_doc, scores, -1000000000.0), axis=-1)
        return jnp.dot(low(attn_prob), values, precision=lax.Precision.HIGHEST)
    attended = lax.map(jax.checkpoint(head_attend), (qkv[0], qkv[1], qkv[2]))
    head_tok = jnp.dot(one_hot, heads_on.astype(jnp.float32), precision=lax.Precision.HIGHEST)
    attended = attended.transpose(1, 0, 2) * head_tok[:, :, None]
    attended = low(low_back(attended.reshape(G_TOK, D)))
    attn_out = low_back(jnp.dot(attended, w_out, precision=lax.Precision.HIGHEST))
    middle = x_rows + gate_a * attn_out
    input_m = low(layer_norm(middle) * (1.0 + scale_m) + shift_m)
    pre_act = low_back(jnp.dot(input_m, w_fc1, precision=lax.Precision.HIGHEST) + b_fc1)
    chan_tok = jnp.repeat(jnp.dot(one_hot, groups_on.astype(jnp.float32), precision=lax.Precision.HIGHEST), FF // CG, axis=1)
    hidden = low(jax.nn.gelu(pre_act, approximate=True) * chan_tok)
    branch = low_back(jnp.dot(hidden, w_fc2, precision=lax.Precision.HIGHEST))
    router = keep_mask.astype(jnp.float32) * jax.nn.sigmoid(logits)
    return middle + gate_m * router[:, None] * branch

def reference(tokens, w_qkv, w_out, w_fc1, b_fc1, w_fc2, null_embed, ada_embed, item_len, null_flag, head_mask, group_mask, token_keep, router_logit, cotangent):

    def forward(x_all, *weights):
        pieces = (x_all.reshape(GROUPS, G_TOK, D), item_len, null_flag, head_mask, group_mask, token_keep.reshape(GROUPS, G_TOK), router_logit.reshape(GROUPS, G_TOK), ada_embed)
        result = lax.map(jax.checkpoint(partial(group_forward, weights)), pieces)
        return result.reshape(TOKENS, D)
    weights = (w_qkv.astype(jnp.float32), w_out.astype(jnp.float32), w_fc1.astype(jnp.float32), b_fc1.astype(jnp.float32), w_fc2.astype(jnp.float32), null_embed.astype(jnp.float32))
    result, pullback = jax.vjp(forward, tokens.astype(jnp.float32), *weights)
    grads = pullback(cotangent.astype(jnp.float32))
    return (result.astype(jnp.bfloat16), grads[0].astype(jnp.bfloat16), grads[1], grads[2], grads[3], grads[4], grads[5], grads[6])
```

```python
import functools

import jax
import jax.numpy as jnp
from jax import lax
from jax.experimental import pallas as pl
from jax.experimental.pallas import tpu as pltpu
from jax.sharding import PartitionSpec as P

HD = 72
SHORT = 256
EPSILON = 1e-06
LOG2E = 1.4426950408889634
GELU_ROOT = 0.7978845608028654
GELU_CUBE = 0.044715
F32 = jnp.float32
BF16 = jnp.bfloat16
MIB = 1 << 20
LANES = 128


def dot(left, right, contract):
    return lax.dot_general(left, right, (contract, ((), ())), preferred_element_type=F32)


NN = ((1,), (0,))
NT = ((1,), (1,))
TN = ((0,), (0,))


def call(body, name, out_shape, scalars, arrays, scratch=(), limit=32):
    vmem = pl.BlockSpec(memory_space=pltpu.VMEM)
    smem = pl.BlockSpec(memory_space=pltpu.SMEM)
    return pl.pallas_call(
        body,
        out_shape=out_shape,
        in_specs=[smem] * len(scalars) + [vmem] * len(arrays),
        out_specs=jax.tree.map(lambda _: vmem, out_shape),
        scratch_shapes=list(scratch),
        compiler_params=pltpu.CompilerParams(vmem_limit_bytes=limit * MIB),
        name=name,
    )(*scalars, *arrays)


def shaped(shape, dtype):
    return jax.ShapeDtypeStruct(tuple(shape), dtype)


def normalize(value):
    center = value - jnp.mean(value, axis=-1, keepdims=True)
    variance = jnp.mean(center * center, axis=-1, keepdims=True)
    inv_std = lax.rsqrt(variance + EPSILON)
    return center * inv_std, inv_std


def norm_back(normed, inv_std, grad_in):
    mean_grad = jnp.mean(grad_in, axis=-1, keepdims=True)
    mean_proj = jnp.mean(grad_in * normed, axis=-1, keepdims=True)
    return inv_std * (grad_in - mean_grad - normed * mean_proj)


def items_body(segments, flags, null_embed, ada, out):
    slots = ada.shape[0]
    for s in range(out.shape[0]):
        item = jnp.minimum(segments[s], slots - 1)
        inside = (segments[s] < slots).astype(F32)
        out[s] = (ada[item] + flags[item].astype(F32) * null_embed[...]) * inside


def qkv_body(index, x, modulation, weight, input_a, out):
    normed, _ = normalize(x[...].astype(F32))
    rows = modulation[index]
    low = (normed * (1.0 + rows[1:2]) + rows[0:1]).astype(BF16)
    input_a[...] = low
    value = dot(low, weight[...], NN).astype(BF16)
    for i in range(value.shape[1] // HD):
        out[:, i * LANES : i * LANES + HD] = value[:, i * HD : (i + 1) * HD]


def chosen(begin, count, size):
    row = lax.broadcasted_iota(jnp.int32, (count, size), 0) + begin
    return (lax.broadcasted_iota(jnp.int32, (count, size), 1) == row).astype(BF16)


def prepare_body(part, where, b_fc1, w_out, wo_part):
    out_cols = wo_part.shape[0] - 16
    wo_part[:out_cols] = dot(chosen(where[0] * out_cols, out_cols, w_out.shape[1]), w_out[...], NT).astype(BF16)
    wo_part[out_cols:] = jnp.zeros((16, wo_part.shape[1]), BF16)
    bias = jnp.broadcast_to(b_fc1[...], (16, b_fc1.shape[1]))
    units = chosen(where[0] * part, part, b_fc1.shape[1])
    wo_part[out_cols:, :part] = dot(bias, units, NT).astype(BF16)


def pack_body(part, where, w_fc1, w_fc2, pack):
    units = chosen(where[0] * part, part, w_fc2.shape[0])
    pack[:part] = dot(units, w_fc1[...], NT).astype(BF16)
    if part % 16 == 0:
        pack[part:] = w_fc2[pl.ds(pl.multiple_of(where[0] * part, 16), part), :]
    else:
        pack[part:] = dot(units, w_fc2[...], NN).astype(BF16)


def column(row):
    size = row.shape[1]
    same = lax.broadcasted_iota(jnp.int32, (size, size), 0) == lax.broadcasted_iota(jnp.int32, (size, size), 1)
    return jnp.sum(jnp.where(same, row, 0.0), axis=1, keepdims=True)


def load_body(cotangent, modulation, keep, logit, chan, payload, router):
    rows = cotangent.shape[0]
    routed = column(keep[...] * jax.nn.sigmoid(logit[...]))
    router[...] = routed
    payload[:rows] = (cotangent[...].astype(F32) * modulation[0, 5:6] * routed).astype(BF16)
    payload[rows:] = jnp.zeros((16, payload.shape[1]), BF16)
    payload[rows:, : chan.shape[1]] = jnp.broadcast_to(chan[...], (16, chan.shape[1])).astype(BF16)


def lay_body(part, *refs):
    weights, (out, biases) = refs[:-2], refs[-2:]
    out_cols, cols = out.shape[0], weights[0].shape[1]
    for s, weight in enumerate(weights):
        out[:, s * cols : (s + 1) * cols] = weight[:out_cols]
        q = (len(weights) - s) % len(weights)
        biases[:, q * part : (q + 1) * part] = weight[out_cols : out_cols + 1, :part].astype(F32)


def rows_of(refs, begin, end):
    found, at = [], 0
    for ref in refs:
        size = ref.shape[0]
        low, high = max(begin - at, 0), min(end - at, size)
        if low < high:
            found.append(ref[low:high])
        at += size
    return jnp.concatenate(found, axis=0) if len(found) > 1 else found[0]


def blocks_of(refs, rows):
    own, from_x, from_y, upper, lower, core = refs
    evens = [[own], [from_x], [from_y], [upper, lower]]
    return [b for i in range(4) for b in (evens[i], [core.at[i * rows : (i + 1) * rows]])]


def flags_body(part, per_quarter, quarters, order, first_group, *refs):
    masks = refs[-1]
    blocks = blocks_of(refs[:-1], refs[0].shape[0])
    units = masks.shape[1]
    quarter = lax.broadcasted_iota(jnp.int32, (1, units), 1) // part
    group = jnp.zeros((1, units), jnp.int32)
    for q in range(quarters):
        group = jnp.where(quarter == q, order[q] * per_quarter + first_group[0], group)
    groups = quarters * per_quarter
    spread = (lax.broadcasted_iota(jnp.int32, (groups, units), 0) == group).astype(BF16)
    end = refs[0].shape[0]
    for m, block in enumerate(blocks):
        chan = rows_of(block, end - 16, end)[:, :groups]
        masks[m : m + 1, :] = dot(chan, spread, NN)[:1]


def place_body(where, *refs):
    weights = refs[-1]
    quarters, width, cols = weights.shape
    out_cols = refs[0].shape[0]
    for m, block in enumerate(blocks_of(refs[:-1], out_cols)):
        at = pl.multiple_of(where[m] * out_cols, 16)
        rows = rows_of(block, 0, out_cols)
        for s in range(quarters):
            weights[s, pl.ds(at, out_cols), :] = rows[:, s * cols : (s + 1) * cols]


def head_of(refs, i):
    return join([r.at[:, i * LANES : i * LANES + HD] for r in refs])


def attend_body(rows, heads, order, segs, head_on, seg_row, *refs):
    blocks = len(refs) - 1
    qkv, out = refs[:blocks], refs[blocks]
    cols = heads * HD
    scale = HD**-0.5 * LOG2E
    bias = jnp.where(seg_row[...] == segs[order], 0.0, -1e30)
    folds = out.shape[1] // cols
    fold_rows = rows // folds
    for h in range(heads):
        q = head_of([qkv[order]], h)
        k = head_of(qkv, heads + h)
        v = head_of(qkv, 2 * heads + h)
        scores = dot(q, k, NT) * scale + bias
        powered = jnp.exp2(scores - jnp.max(scores, axis=1, keepdims=True))
        total = jnp.sum(powered, axis=1, keepdims=True)
        mixed = dot(powered.astype(BF16), v, NN) * (head_on[order, h] / total)
        mixed = mixed.astype(BF16)
        for f in range(folds):
            out[:, f * cols + h * HD : f * cols + (h + 1) * HD] = mixed[f * fold_rows : (f + 1) * fold_rows]


def unfold(ref, cols):
    folds = ref.shape[1] // cols
    return jnp.concatenate([ref[:, f * cols : (f + 1) * cols] for f in range(folds)], axis=0)


def project_body(cols, tokens, modulation, weight, *refs):
    pieces, (attn_out, middle, input_m) = refs[:-3], refs[-3:]
    rows = modulation[0]
    total = 0.0
    for s, piece in enumerate(pieces):
        total = total + dot(unfold(piece, cols), weight[s], NT)
    attn_out[...] = total
    value = tokens[...].astype(F32) + rows[2:3] * total
    middle[...] = value
    normed, _ = normalize(value)
    input_m[...] = (normed * (1.0 + rows[4:5]) + rows[3:4]).astype(BF16)


def join(refs):
    return jnp.concatenate([r[...] for r in refs], axis=0) if len(refs) > 1 else refs[0][...]


def unpack(packs, part):
    w1 = jnp.concatenate([r[:part] for r in packs], axis=0)
    w2 = jnp.concatenate([r[part : 2 * part] for r in packs], axis=0)
    return w1, w2


def mlp_body(sizes, quarters, part, picks, masks, bias, *refs):
    packs = refs[:quarters]
    refs = refs[quarters:]
    count = sum(sizes)
    xs, refs = refs[:count], refs[count:]
    outs = refs[-2 - len(sizes) : -2]
    hidden_ref, grad_ref = refs[-2:]
    rows = outs[0].shape[0]
    givens = refs[: -2 - len(sizes)]
    givens = [[g] for g in givens] if len(givens) == 1 else blocks_of(givens, givens[0].shape[0])
    w1, w2 = unpack(packs, part)
    begin = 0
    for b, size in enumerate(sizes):
        x, g = join(xs[begin : begin + size]), rows_of(givens[picks[b]], 0, rows)
        begin += size
        mask = masks[picks[b] : picks[b] + 1, :]
        v = dot(x, w1, NT) + bias[...]
        grad_hidden = dot(g, w2, NT)
        square = v * v
        t = jnp.tanh(GELU_ROOT * v * (1.0 + GELU_CUBE * square))
        half = 0.5 * (1.0 + t)
        slope = half + 0.5 * v * (1.0 - t * t) * (GELU_ROOT * (1.0 + 3.0 * GELU_CUBE * square))
        hidden_ref[b * rows : (b + 1) * rows, :] = (v * half * mask).astype(BF16)
        grad_pre = (grad_hidden * mask * slope).astype(BF16)
        grad_ref[b * rows : (b + 1) * rows, :] = grad_pre
        outs[b][...] = dot(grad_pre, w1, NN).astype(BF16)


def branch_body(quarters, part, count, *refs):
    _, w2 = unpack(refs[:quarters], part)
    hiddens, (keep, send) = refs[quarters : quarters + count], refs[quarters + count :]
    rows = keep.shape[1]
    b = 0
    for hidden in hiddens:
        for i in range(hidden.shape[0] // rows):
            (send if b % 2 else keep)[b // 2] = dot(hidden[i * rows : (i + 1) * rows, :], w2, NN).astype(BF16)
            b += 1


def split_rows(where, total, keep, send):
    size = keep.shape[1]
    for m in range(2 * keep.shape[0]):
        at = pl.multiple_of(where[m] * size, 16)
        (send if m % 2 else keep)[m // 2] = total[pl.ds(at, size), :].astype(BF16)


def fold_body(cut, count, whole, *refs):
    outs = list(refs[2 * count :])
    for i in range(count):
        total = (refs[i][...].astype(F32) + refs[count + i][...].astype(F32)).astype(BF16)
        if i < whole:
            outs.pop(0)[...] = total
        else:
            outs.pop(0)[...] = total[:cut]
            outs.pop(0)[...] = total[cut:]


def fc_grad_body(count, split, rows, quarters, *refs):
    acts, given, outs, sums = refs[:count], refs[count : -1 - quarters], refs[-1 - quarters : -1], refs[-1]
    if split:
        blocks = [rows_of(b, 0, rows) for b in blocks_of(given, given[0].shape[0])]
    else:
        blocks = [ref[...] for ref in given]
    given = jnp.concatenate(blocks, axis=0)
    acc, total, begin = 0.0, 0.0, 0
    for act in acts:
        size = act.shape[0]
        acc = acc + dot(act[...], given[begin : begin + size], TN)
        total = total + jnp.sum(act[...].astype(F32), axis=0, keepdims=True)
        begin += size
    sums[...] = total
    part = outs[0].shape[0]
    for s, out in enumerate(outs):
        out[...] = acc[s * part : (s + 1) * part].astype(BF16)


def fc_turn_body(first, first_in, second, second_in, out):
    part, size = first.shape[0], out.shape[1]
    pairs = ((first[...].astype(F32) + first_in[...].astype(F32)), (second[...].astype(F32) + second_in[...].astype(F32)))
    for i, total in enumerate(pairs):
        low = total.astype(BF16)
        for d in range(out.shape[0]):
            out[d, :, i * part : (i + 1) * part] = low[:, d * size : (d + 1) * size].T


def fc_leave_body(given, first, second):
    part = given.shape[2] // 2
    for d in range(given.shape[0]):
        first[:, d * part : (d + 1) * part] = given[d, :, :part].astype(F32)
        second[d * part : (d + 1) * part, :] = given[d, :, part:].astype(F32).T


def total_of(begins, takes, refs):
    whole = refs[0][...].astype(F32)
    rows = whole.shape[0]
    for begin, take, ref in zip(begins[1:], takes[1:], refs[1:]):
        take = ref.shape[0] if take is None else take
        piece = ref[:take].astype(F32)
        if take < rows:
            blank = [jnp.zeros((n, piece.shape[1]), F32) for n in (begin, rows - begin - take)]
            piece = jnp.concatenate([b for b in (blank[0], piece, blank[1]) if b.shape[0]], axis=0)
        whole = whole + piece
    return whole


def middle_back_body(cols, begins, cotangent, modulation, middle, attn_out, weight, *refs):
    count = len(begins)
    grad_middle, grad_attn, sums = refs[count : count + 3]
    pieces = refs[count + 3 :]
    grad_in = total_of(begins, [None] * count, refs[:count])
    rows = modulation[0]
    normed, inv_std = normalize(middle[...])
    grad = cotangent[...].astype(F32) + norm_back(normed, inv_std, grad_in * (1.0 + rows[4:5]))
    grad_middle[...] = grad
    sums[0:1] = jnp.sum(grad * attn_out[...], axis=0, keepdims=True)
    sums[1:2] = jnp.sum(grad_in, axis=0, keepdims=True)
    sums[2:3] = jnp.sum(grad_in * normed, axis=0, keepdims=True)
    low = (grad * rows[2:3]).astype(BF16)
    grad_attn[...] = low
    folds = pieces[0].shape[1] // cols
    fold_rows = low.shape[0] // folds
    for s, piece in enumerate(pieces):
        value = dot(low, weight[s], NN).astype(BF16)
        for f in range(folds):
            piece[:, f * cols : (f + 1) * cols] = value[f * fold_rows : (f + 1) * fold_rows]


def attend_back_body(rows, heads, segs, head_on, seg_col, *refs):
    blocks = (len(refs) - 2) // 3
    qkv, grads, outs = refs[:blocks], refs[blocks : 2 * blocks], refs[2 * blocks : 3 * blocks]
    dk_ref, dv_ref = refs[3 * blocks :]
    cols = heads * HD
    scale = HD**-0.5 * LOG2E
    given = [unfold(g, cols) for g in grads]
    for i in range(blocks):
        bias = jnp.where(seg_col[...] == segs[i], 0.0, -1e30)
        for h in range(heads):
            q = head_of([qkv[i]], h)
            k = head_of(qkv, heads + h)
            v = head_of(qkv, 2 * heads + h)
            g = (given[i][:, h * HD : (h + 1) * HD].astype(F32) * head_on[i, h]).astype(BF16)
            scores = dot(k, q, NT) * scale + bias
            powered = jnp.exp2(scores - jnp.max(scores, axis=0, keepdims=True))
            prob = powered * (1.0 / jnp.sum(powered, axis=0, keepdims=True))
            grad_prob = dot(v, g, NT)
            inner = jnp.sum(prob * grad_prob, axis=0, keepdims=True)
            grad_score = (prob * (grad_prob - inner)).astype(BF16)
            dv = dot(prob.astype(BF16), g, NN)
            dk = dot(grad_score, q, NN)
            dq = dot(grad_score, k, TN)
            outs[i][:, h * HD : (h + 1) * HD] = (dq * HD**-0.5).astype(BF16)
            dk_ref[h] = dk if i == 0 else dk_ref[h] + dk
            dv_ref[h] = dv if i == 0 else dv_ref[h] + dv
    for h in range(heads):
        for i in range(blocks):
            dk = dk_ref[h, i * rows : (i + 1) * rows, :] * HD**-0.5
            dv = dv_ref[h, i * rows : (i + 1) * rows, :]
            outs[i][:, cols + h * HD : cols + (h + 1) * HD] = dk.astype(BF16)
            outs[i][:, 2 * cols + h * HD : 2 * cols + (h + 1) * HD] = dv.astype(BF16)


def qkv_grads_body(blocks, where, *refs):
    xs, gs = refs[:blocks], refs[blocks : 2 * blocks]
    outs, total = refs[2 * blocks : -1], refs[-1]
    acc = 0.0
    for x, g in zip(xs, gs):
        acc = acc + dot(x[...], g[...], TN)
    if len(outs) == 1:
        outs[0][...] = acc.astype(BF16)
        return
    total[...] = acc
    split_rows(where, total, *outs)


def out_grads_body(cols, blocks, where, grad, *refs):
    outs, total = refs[blocks:-1], refs[-1]
    for s, piece in enumerate(refs[:blocks]):
        total[:, s * cols : (s + 1) * cols] = dot(grad[...], unfold(piece, cols), TN)
    if len(outs) == 1:
        outs[0][...] = total[...].astype(BF16)
        return
    split_rows(where, total, *outs)


def fold_near_body(cut, keep, got, own, for_x, for_y, send_x, send_y):
    rows = own.shape[0]
    blocks = [(keep[i].astype(F32) + got[i].astype(F32)).astype(BF16) for i in range(4)]
    own[...] = blocks[0]
    for_x[...] = blocks[1][cut:]
    for_y[...] = blocks[2][:cut]
    send_x[:cut] = blocks[1][:cut]
    send_x[cut:] = blocks[3][:cut]
    send_y[: rows - cut] = blocks[2][cut:]
    send_y[rows - cut :] = blocks[3][cut:]


def out_sum_body(begins, takes, *refs):
    total = total_of(begins, takes, refs[: len(begins)])
    pieces = refs[len(begins) :]
    cols = pieces[0].shape[1]
    for s, piece in enumerate(pieces):
        piece[...] = total[:, s * cols : (s + 1) * cols].astype(BF16)


def qkv_leave_body(begins, takes, *refs):
    total = total_of(begins, takes, refs[:-1])
    cols = refs[-1].shape[2]
    for i in range(3):
        refs[-1][:, i, :] = total[:, i * cols : (i + 1) * cols]


def leave_body(begins, takes, cotangent, router, modulation, middle, *refs):
    count = len(begins)
    output, sums = refs[count:]
    routed = router[...] * total_of(begins, takes, refs[:count])
    output[...] = (middle[...] + modulation[0, 5:6] * routed).astype(BF16)
    sums[...] = jnp.sum(cotangent[...].astype(F32) * routed, axis=0, keepdims=True)


def null_body(flags, *refs):
    count = (len(refs) - 1) // 2
    xs, parts, out = refs[:count], refs[count : 2 * count], refs[-1]
    first, second = 0.0, 0.0
    for s in range(count):
        normed, _ = normalize(xs[s][...].astype(F32))
        grad = parts[s][...].astype(F32) * flags[s]
        first = first + jnp.sum(grad, axis=0, keepdims=True)
        second = second + jnp.sum(grad * normed, axis=0, keepdims=True)
    out[0:1] = first
    out[1:2] = second


def token_back_body(tokens, modulation, grad_middle, own, received, grad_tokens):
    normed, inv_std = normalize(tokens[...].astype(F32))
    grad_in = own[...].astype(F32) + received[...].astype(F32)
    grad = grad_middle[...] + norm_back(normed, inv_std, grad_in * (1.0 + modulation[0, 1:2]))
    grad_tokens[...] = grad.astype(BF16)


def after(value, *others):
    return lax.optimization_barrier((value, others))[0]


def together(*values):
    return lax.optimization_barrier(values)


def shift(value, axis, size, step):
    return lax.ppermute(value, axis, [(i, (i + step) % size) for i in range(size)])


def swap(value, axis, size, bit):
    return lax.ppermute(value, axis, [(i, i ^ bit) for i in range(size)])


def ring_gather(block, axis, size):
    blocks = [block]
    for _ in range(size - 1):
        blocks.append(shift(blocks[-1], axis, size, 1))
    return blocks


def ring_reduce(parts, axis, size):
    total = parts[1 % size]
    for step in range(2, size + 1):
        total = shift(total, axis, size, 1)
        if step < size:
            total = total + parts[step]
    return parts[0], total


def cube_gather(block, axis, size):
    block = block[None]
    bit = 1
    while bit < size:
        block = jnp.concatenate([block, swap(block, axis, size, bit)], axis=0)
        bit *= 2
    return block


def cube_sum(value, axis, size):
    bit = 1
    while bit < size:
        value = value + swap(value, axis, size, bit)
        bit *= 2
    return value


def shift_all(parts, axis, size, sign):
    return [parts[0]] + [shift(parts[s], axis, size, sign * s) for s in range(1, size)]


def far(from_x, from_y, cut):
    return [swap(from_y[:cut], "dp", 8, 2), swap(from_x[cut:], "dp", 8, 4)]


def with_core(blocks):
    return [*blocks, swap(jnp.concatenate(blocks, axis=0), "dp", 8, 1)]


def fold(name, pairs, cut):
    rows, cols = pairs[0][0].shape
    return call(
        functools.partial(fold_body, cut, len(pairs), 0),
        name,
        tuple([shaped((cut, cols), BF16), shaped((rows - cut, cols), BF16)] * len(pairs)),
        [],
        [a for a, _ in pairs] + [b for _, b in pairs],
    )


def reduce_near(name, keep, got, cut):
    _, rows, cols = keep.shape
    sizes = (rows, rows - cut, cut, 2 * cut, 2 * (rows - cut))
    own, for_x, for_y, send_x, send_y = call(
        functools.partial(fold_near_body, cut),
        name,
        tuple(shaped((n, cols), BF16) for n in sizes),
        [],
        [keep, got],
    )
    return [own, for_x, for_y, swap(send_x, "dp", 8, 2), swap(send_y, "dp", 8, 4)]


def reduce_far(state):
    own, for_x, for_y, got_x, got_y = state
    cut, rest = for_y.shape[0], for_x.shape[0]
    last_x, last_y = for_x + got_y[rest:], for_y + got_x[cut:]
    arrays = [own, got_x, swap(last_x, "dp", 8, 2), swap(last_y, "dp", 8, 4), got_y]
    return [0, 0, cut, 0, cut], [None, cut, None, None, rest], arrays, [last_x, last_y]


def local(
    tokens,
    w_qkv,
    w_out,
    w_fc1,
    b_fc1,
    w_fc2,
    null_embed,
    ada_embed,
    item_len,
    null_flag,
    head_mask,
    group_mask,
    token_keep,
    router_logit,
    cotangent,
):
    n_tensor = lax.axis_size("tensor")
    n_dp = lax.axis_size("dp")
    z = lax.axis_index("tensor")
    p = lax.axis_index("dp")
    rows, width = tokens.shape
    group_rows = rows * n_tensor
    local_cols = w_qkv.shape[2]
    local_heads = local_cols // HD
    local_hidden = w_fc1.shape[1]
    part = local_hidden // n_dp
    hidden_units = part * n_tensor
    out_cols = width // n_dp
    slots = item_len.shape[1]
    chan_size = local_hidden * n_tensor // group_mask.shape[2]
    local_groups = group_mask.shape[2] // n_tensor
    folds = 4
    assert SHORT % rows == 0 and chan_size % part == 0 and n_dp & (n_dp - 1) == 0
    piece_shape = shaped((rows // folds, folds * local_cols), BF16)
    block_shape = shaped((rows, width), BF16)

    cube = n_dp == 8 and n_tensor == 4
    payload_rows = rows + 16
    cut = payload_rows // 2 // 16 * 16
    half = rows // 2
    out_cut = out_cols // 2 // 16 * 16
    lengths, flags = item_len[0], null_flag[0]

    rows_x = [tokens, shift(tokens, "tensor", n_tensor, 1)]
    mine_index = p[None].astype(jnp.int32)
    wo_part = call(
        functools.partial(prepare_body, part),
        "prepare",
        shaped((out_cols + 16, local_cols), BF16),
        [mine_index],
        [b_fc1[None], w_out],
    )
    wo_mine = shift_all([wo_part] * n_tensor, "tensor", n_tensor, -1)
    peers = (p ^ jnp.arange(n_dp)).astype(jnp.int32)
    order = ((z - jnp.arange(n_tensor)) % n_tensor).astype(jnp.int32)
    first_group = (p * part // chan_size)[None].astype(jnp.int32)

    starts = order * rows
    ends = jnp.sum(jnp.where(jnp.arange(slots)[:, None] >= jnp.arange(slots)[None, :], lengths[None, :], 0), axis=1)
    segments = jnp.sum((ends[None, :] <= starts[:, None]).astype(jnp.int32), axis=1)
    hot = (segments[:, None] == jnp.arange(slots)[None, :]).astype(F32)
    heads_here = lax.dynamic_slice_in_dim(head_mask[0], z * local_heads, local_heads, 1).astype(F32)
    head_on = jnp.sum(hot[:, :, None] * heads_here[None], axis=1)
    seg_rows = jnp.repeat(segments, rows)
    nulls = jnp.sum(hot * flags.astype(F32)[None], axis=1)
    my_chan = jnp.sum(hot[0][:, None] * group_mask[0].astype(F32), axis=0)[None]
    modulation = call(
        items_body,
        "items",
        shaped((n_tensor, 6, width), F32),
        [segments, flags],
        [null_embed, ada_embed[0]],
    )
    payload, router = call(
        load_body,
        "load",
        (shaped((payload_rows, width), BF16), shaped((rows, 1), F32)),
        [],
        [cotangent, modulation, token_keep.astype(F32)[None], router_logit[None], my_chan],
    )
    wo_flat, biases = call(
        functools.partial(lay_body, part),
        "lay",
        (shaped((out_cols, width), BF16), shaped((1, hidden_units), F32)),
        [],
        wo_mine,
    )
    flat_qkv = w_qkv.reshape(width, 3 * local_cols)

    def project_in(s, block):
        return call(
            functools.partial(qkv_body, s),
            f"qkv_{s}",
            (block_shape, shaped((rows, 3 * local_heads * LANES), BF16)),
            [],
            [block, modulation, flat_qkv],
        )

    rows_x[1], payload, wo_flat = together(rows_x[1], payload, wo_flat)
    rows_x.append(shift(rows_x[1], "tensor", n_tensor, 1))
    if cube:
        pay_x, pay_y = swap(payload, "dp", n_dp, 2), swap(payload, "dp", n_dp, 4)
    pack = call(
        functools.partial(pack_body, part),
        "pack",
        shaped((2 * part, width), BF16),
        [after(mine_index, payload)],
        [w_fc1, w_fc2],
    )
    input_a, qkv = zip(project_in(0, after(rows_x[0], payload)), project_in(1, rows_x[1]))
    input_a, qkv = [*input_a], [*qkv]
    rows_x[2], pack, qkv = together(rows_x[2], pack, qkv)
    for s in range(2, n_tensor):
        if s + 1 < n_tensor:
            rows_x.append(shift(rows_x[s], "tensor", n_tensor, 1))
        if cube and s == 2:
            pay_x, pay_y, wo_flat = together(*after((pay_x, pay_y), rows_x[2]), wo_flat)
            pay_far = far(pay_x, pay_y, cut)
            wo_x, wo_y = swap(wo_flat, "dp", n_dp, 2), swap(wo_flat, "dp", n_dp, 4)
        low, value = project_in(s, rows_x[s])
        input_a.append(low)
        qkv.append(value)
        if cube and s == 2:
            rows_x[3], value, pay_far = together(rows_x[3], value, pay_far)
            qkv[2] = value
        elif s + 1 < n_tensor:
            rows_x[s + 1] = after(rows_x[s + 1], value)
    pack = after(pack, rows_x[-1])
    packs = [pack, shift(pack, "tensor", n_tensor, 1)]
    if cube:
        payloads = with_core([payload, pay_x, pay_y, *pay_far])
        wo_far = far(*after((wo_x, wo_y), rows_x[-1]), out_cut)

    def attend(s, qkv):
        return call(
            functools.partial(attend_body, rows, local_heads, s),
            f"attend_{s}",
            piece_shape,
            [segments, head_on],
            [seg_rows[None, :], *qkv],
        )

    pieces, mine = {}, {}
    away = [n_tensor // 2] + [s for s in range(1, n_tensor) if s != n_tensor // 2]
    for step, s in enumerate([*away, 0]):
        pieces[s] = attend(s, qkv)
        qkv = after(qkv, pieces[s])
        if step == 0 and cube:
            pieces[s], wo_far, payloads, qkv = together(pieces[s], wo_far, payloads, qkv)
            wo_blocks = with_core([wo_flat, wo_x, wo_y, *wo_far])
        mine[s] = shift(pieces[s], "tensor", n_tensor, -s) if s else pieces[s]
    if cube:
        masks = call(
            functools.partial(flags_body, part, local_groups, n_tensor),
            "flags",
            shaped((n_dp, hidden_units), F32),
            [order, first_group],
            after(payloads, pieces[0]),
        )
        wo_all = call(
            place_body,
            "place",
            shaped((n_tensor, width, local_cols), BF16),
            [peers],
            after(wo_blocks, masks),
        )
    else:
        wo_all = lax.all_gather(wo_flat, "dp", axis=0).reshape(n_dp, out_cols, n_tensor, local_cols)
        wo_all = wo_all.transpose(2, 0, 1, 3).reshape(n_tensor, width, local_cols)
        payloads = lax.all_gather(payload, "dp", axis=0)
        chan = payloads[:, rows, : n_tensor * local_groups].astype(F32)
        chan = chan.reshape(n_dp, n_tensor, local_groups)
        chan = lax.dynamic_index_in_dim(chan, first_group[0], 2, False)[:, order]
        masks = jnp.repeat(chan, part, axis=1)
    mine = [mine[s] for s in range(n_tensor)]
    mine, packs[1], wo_all = together(mine, packs[1], wo_all)
    packs.append(shift(packs[1], "tensor", n_tensor, 1))
    attn_out, middle, input_m = call(
        functools.partial(project_body, local_cols),
        "project",
        (shaped((rows, width), F32), shaped((rows, width), F32), block_shape),
        [],
        [tokens, modulation, wo_all, *mine],
    )

    def mlp(name, picks, masks, xs, gs):
        acts = shaped((len(xs) * rows, hidden_units), BF16)
        return call(
            functools.partial(mlp_body, [len(x) for x in xs], n_tensor, part, picks),
            name,
            (*[block_shape] * len(xs), acts, acts),
            [],
            [masks, biases, *packs, *sum(xs, []), *gs],
        )

    def fc_grad(name, acts, arrays, split):
        *outs, sums = call(
            functools.partial(fc_grad_body, len(acts), split, rows, n_tensor),
            name,
            (*[shaped((part, width), BF16)] * n_tensor, shaped((1, hidden_units), F32)),
            [],
            [*acts, *arrays],
        )
        return outs, sums

    if cube:
        core, from_x, from_y = [swap(input_m, "dp", n_dp, bit) for bit in (1, 2, 4)]
        core, from_x, from_y, packs[2] = together(core, from_x, from_y, packs[2])
        packs.append(shift(packs[2], "tensor", n_tensor, 1))
        upper, lower = far(from_x, from_y, half)
        from_xc, from_yc = swap(from_x, "dp", n_dp, 1), swap(from_y, "dp", n_dp, 1)
        *part_a, hidden_a, pre_a = mlp("mlp_0", (0, 1), masks, [[input_m], [core]], payloads)
        near_x, upper, lower = together([from_x, from_xc, from_y, from_yc], upper, lower)
        near_x = after(near_x, hidden_a)
        own = [part_a[0], swap(part_a[1], "dp", n_dp, 1)]
        upper_c, lower_c = swap(upper, "dp", n_dp, 1), swap(lower, "dp", n_dp, 1)
        *part_b, hidden_b, pre_b = mlp("mlp_2", (2, 3, 4, 5), masks, [[b] for b in near_x], payloads)
        own, upper_c, lower_c = together(own, upper_c, lower_c)
        part_b = [(part_b[m], swap(part_b[m + 1], "dp", n_dp, 1)) for m in (0, 2)]
        x_upper, x_lower, y_upper, y_lower = fold("fold_b", part_b, half)
        far_x = after([upper, lower, upper_c, lower_c], x_lower)
        x_upper, y_lower = swap(x_upper, "dp", n_dp, 2), swap(y_lower, "dp", n_dp, 4)
        *part_c, hidden_c, pre_c = mlp("mlp_6", (6, 7), masks, [far_x[:2], far_x[2:]], payloads)
        cross = fold("fold_c", [(part_c[0], swap(part_c[1], "dp", n_dp, 1))], half)
        hiddens, grad_pres = [hidden_a, hidden_b, hidden_c], [pre_a, pre_b, pre_c]
        rows_m = [input_m, core, *near_x, upper, lower, upper_c, lower_c]
        rows_m[2:6] = near_x
        via_x, via_y = swap(cross[0], "dp", n_dp, 2), swap(cross[1], "dp", n_dp, 4)
        grad_fc2, _ = fc_grad("fc2_grad", after(hiddens, cross), payloads, True)
        via_x, via_y, x_upper, y_lower = after((via_x, via_y, x_upper, y_lower), grad_fc2)
        last_x, last_y = x_lower + via_y, y_upper + via_x
        last_x, last_y, x_upper, y_lower = together(last_x, last_y, x_upper, y_lower)
        x_lower, y_upper = swap(last_x, "dp", n_dp, 2), swap(last_y, "dp", n_dp, 4)
        fc2_total = shift(after(grad_fc2[1], last_x), "tensor", n_tensor, 1)
        grad_fc1, grad_bias = fc_grad("fc1_grad", after(grad_pres, last_x, last_y), rows_m, False)
        grad_in_m = [*own, x_upper, x_lower, y_upper, y_lower]
        begins = [0, 0, 0, half, 0, half]
        grad_in_m, fc2_total, fc1_first = together(grad_in_m, fc2_total, grad_fc1[1])
        fc2_total = fc2_total + grad_fc2[2 % n_tensor]
        fc2_total = shift(fc2_total, "tensor", n_tensor, 1)
    else:
        while len(packs) < n_tensor:
            packs.append(shift(packs[-1], "tensor", n_tensor, 1))
        rows_m = lax.all_gather(input_m, "dp", axis=0)

        def step(sums, given):
            x, g, m = given
            out, hidden, grad_pre = mlp("mlp", (0,), m[None], [[x]], [g])
            sums = [a + dot(b, c, TN) for a, b, c in zip(sums, (grad_pre, hidden), (x, g[:rows]))]
            return sums, (out, hidden, jnp.sum(grad_pre.astype(F32), axis=0, keepdims=True))

        zero = jnp.zeros((hidden_units, width), F32)
        sums, (grad_parts, hidden, grad_bias) = lax.scan(step, [zero, zero], (rows_m, payloads, masks))
        begins, grad_in_m = [0], [lax.psum_scatter(grad_parts, "dp", scatter_dimension=0)]
        grad_bias = jnp.sum(grad_bias, axis=0)
        sums = [a.astype(BF16).reshape(n_tensor, part, width) for a in sums]
        grad_fc1, grad_fc2 = [[a[s] for s in range(n_tensor)] for a in sums]
        fc2_total = shift(grad_fc2[1], "tensor", n_tensor, 1) + grad_fc2[2 % n_tensor]
        fc2_total, fc1_total = [shift(t, "tensor", n_tensor, 1) for t in (fc2_total, grad_fc1[1])]

    grad_middle, grad_attn, sums_m, *grad_pieces = call(
        functools.partial(middle_back_body, local_cols, begins),
        "middle_back",
        (shaped((rows, width), F32), block_shape, shaped((3, width), F32), *[piece_shape] * n_tensor),
        [],
        [cotangent, modulation, middle, attn_out, wo_all, *grad_in_m],
    )
    grads = shift_all(grad_pieces, "tensor", n_tensor, 1)
    late_attn = after(grad_attn, grad_pieces)

    if cube:
        branch_keep, branch_send = call(
            functools.partial(branch_body, n_tensor, part, len(hiddens)),
            "branch",
            tuple([shaped((n_dp // 2, rows, width), BF16)] * 2),
            [],
            [*packs, *after(hiddens, late_attn)],
        )
        branch_got = swap(branch_send, "dp", n_dp, 1)
        late_attn = after(late_attn, branch_keep)
    grad_wout = call(
        functools.partial(out_grads_body, local_cols, n_tensor),
        "out_grads",
        (shaped((4, out_cols, width), BF16),) * 2 if cube else (shaped((width, width), BF16),),
        [peers],
        [late_attn, *mine],
        scratch=[pltpu.VMEM((width, width), F32)],
    )
    if cube:
        grads, branch_got, grad_wout, fc2_total = together(grads, branch_got, grad_wout, fc2_total)
        wout_got = swap(grad_wout[1], "dp", n_dp, 1)
        branch_state = reduce_near("branch_near", branch_keep, branch_got, half)
        fc2_total = shift(fc2_total + grad_fc2[3], "tensor", n_tensor, 1)
        fc1_total = shift(fc1_first, "tensor", n_tensor, 1)
        grads = after(grads, branch_state[0])
    else:
        fc2_total, fc1_total = fc2_total + grad_fc2[3 % n_tensor], fc1_total + grad_fc1[2 % n_tensor]
        fc2_total, fc1_total = [shift(t, "tensor", n_tensor, 1) for t in (fc2_total, fc1_total)]
        w2 = jnp.concatenate([r[part:] for r in packs], axis=0)
        branch = after(hidden, grad_fc1).reshape(n_dp * rows, hidden_units)
        branch = dot(branch, w2, NN).astype(BF16).reshape(n_dp, rows, width)
        late_begins, takes, branch = [0], [None], [lax.psum_scatter(branch, "dp", scatter_dimension=0)]
        wout_sum = lax.psum_scatter(grad_wout[0].reshape(n_dp, out_cols, width), "dp", scatter_dimension=0)

    grad_rows = call(
        functools.partial(attend_back_body, rows, local_heads),
        "attend_back",
        tuple([shaped((rows, 3 * local_cols), BF16)] * n_tensor),
        [segments, head_on],
        [seg_rows[:, None], *qkv, *grads],
        scratch=[pltpu.VMEM((local_heads, group_rows, HD), F32)] * 2,
        limit=48,
    )
    first = dot(grad_rows[1], flat_qkv, NT).astype(BF16)
    later = grad_rows
    if cube:
        first, branch_state, wout_got, fc2_total, fc1_total = together(
            first, branch_state, wout_got, fc2_total, fc1_total
        )
        total = shift(first, "tensor", n_tensor, 1)
        late_begins, takes, branch, marks = reduce_far(branch_state)
        wout_state = reduce_near("wout_near", *after((grad_wout[0], wout_got), marks), out_cut)
        later = after(grad_rows, wout_state[0])
    else:
        total = shift(first, "tensor", n_tensor, 1)
    grad_in_parts = [dot(later[s], flat_qkv, NT).astype(BF16) if s != 1 else first for s in range(n_tensor)]
    grad_wqkv = call(
        functools.partial(qkv_grads_body, n_tensor),
        "qkv_grads",
        tuple([shaped((4, out_cols, 3 * local_cols), BF16)] * 2)
        if cube
        else (shaped((width, 3 * local_cols), BF16),),
        [peers],
        [*input_a, *after(later, grad_in_parts)],
        scratch=[pltpu.VMEM((width, 3 * local_cols), F32)],
    )
    if cube:
        grad_wqkv, branch, wout_state = together(grad_wqkv, branch, wout_state)
        wout_begins, wout_takes, wout_last, marks = reduce_far(wout_state)
        qkv_got = swap(grad_wqkv[1], "dp", n_dp, 1)
        fc1_total = fc1_total + grad_fc1[2]
        fc1_total = shift(fc1_total, "tensor", n_tensor, 1)
        total, wout_last, qkv_got, fc1_total = together(total, wout_last, qkv_got, fc1_total)
    for s in range(2, n_tensor):
        total = total + grad_in_parts[s]
        mark = total
        total = shift(total, "tensor", n_tensor, 1)
        if s > 2:
            continue
        if cube:
            fc1_total = shift(fc1_total + grad_fc1[3], "tensor", n_tensor, 1)
            qkv_state = reduce_near("qkv_near", *after((grad_wqkv[0], qkv_got), mark), out_cut)
            branch = after(branch, qkv_state[0])
            wout_parts = call(
                functools.partial(out_sum_body, wout_begins, wout_takes),
                "out_sum",
                tuple([shaped((out_cols, local_cols), BF16)] * n_tensor),
                [],
                after(wout_last, qkv_state[0]),
            )
        else:
            wout_parts = [wout_sum[:, i * local_cols : (i + 1) * local_cols] for i in range(n_tensor)]
        wout_ring = [wout_parts[(n_tensor - i) % n_tensor] for i in range(n_tensor)]
        wout_total = shift(wout_ring[1], "tensor", n_tensor, 1)
        output, sums_b = call(
            functools.partial(leave_body, late_begins, takes),
            "leave",
            (block_shape, shaped((1, width), F32)),
            [],
            [cotangent, router, modulation, middle, *(after(branch, wout_parts) if cube else branch)],
        )
        sums_a = call(
            null_body,
            "null",
            shaped((2, width), F32),
            [nulls],
            [*after(rows_x, sums_b), *grad_in_parts],
        )
        bias_full = lax.dynamic_update_slice_in_dim(
            jnp.zeros((n_tensor, local_hidden), F32), grad_bias.reshape(n_tensor, part)[order], p * part, 1
        )
        small = jnp.concatenate(
            [bias_full.reshape(-1, width), sums_a, nulls[0] * sums_m, nulls[0] * sums_b], axis=0
        )
        if cube:
            total, small, wout_total, qkv_state, fc1_total = together(
                total, small, wout_total, qkv_state, fc1_total
            )
    wout_total = shift(wout_total + wout_ring[2 % n_tensor], "tensor", n_tensor, 1)
    if not cube:
        fc1_total = shift(fc1_total + grad_fc1[3 % n_tensor], "tensor", n_tensor, 1)
    for s in range(4, n_tensor):
        fc2_total = shift(fc2_total + grad_fc2[s], "tensor", n_tensor, 1)
        fc1_total = shift(fc1_total + grad_fc1[s], "tensor", n_tensor, 1)
    for s in range(3, n_tensor):
        wout_total = shift(wout_total + wout_ring[s], "tensor", n_tensor, 1)

    fc1_total = after(fc1_total, mark)
    fc_sum = call(
        fc_turn_body,
        "fc_turn",
        shaped((n_dp, out_cols, 2 * part), BF16),
        [],
        [grad_fc1[0], fc1_total, grad_fc2[0], fc2_total],
    )
    if cube:
        qkv_begins, qkv_takes, qkv_last, _ = reduce_far(after(qkv_state, mark))
    else:
        qkv_begins, qkv_takes = [0], [None]
        qkv_last = grad_wqkv[0].reshape(n_dp, out_cols, 3 * local_cols)
        qkv_last = [lax.psum_scatter(qkv_last, "dp", scatter_dimension=0)]
    fc_sum = lax.all_to_all(fc_sum, "dp", split_axis=0, concat_axis=0)
    small = cube_sum(small, "dp", n_dp)
    small = cube_sum(small, "tensor", n_tensor)
    qkv_sum = call(
        functools.partial(qkv_leave_body, qkv_begins, qkv_takes),
        "qkv_leave",
        shaped((out_cols, 3, local_cols), F32),
        [],
        qkv_last,
    )
    fc1_sum, fc2_sum = call(
        fc_leave_body,
        "fc_leave",
        (shaped((out_cols, local_hidden), F32), shaped((local_hidden, out_cols), F32)),
        [],
        [fc_sum],
    )
    wout_sum = (wout_ring[0].astype(F32) + wout_total.astype(F32)).T
    bias_sum, null_sum = small[:-6].reshape(-1), small[-6:]
    grad_tokens = call(
        token_back_body,
        "token_back",
        block_shape,
        [],
        [tokens, modulation, grad_middle, grad_in_parts[0], total],
    )

    return (
        output,
        grad_tokens,
        qkv_sum,
        wout_sum,
        fc1_sum,
        bias_sum,
        fc2_sum,
        null_sum,
    )


def solution(mesh):
    in_specs = (
        P(("dp", "tensor"), None),
        P(None, None, "tensor"),
        P("tensor", None),
        P(None, "tensor"),
        P("tensor"),
        P("tensor", None),
        P(),
        P("dp", None, None, None),
        P("dp", None),
        P("dp", None),
        P("dp", None, None),
        P("dp", None, None),
        P(("dp", "tensor")),
        P(("dp", "tensor")),
        P(("dp", "tensor"), None),
    )
    out_specs = (
        P(("dp", "tensor"), None),
        P(("dp", "tensor"), None),
        P("dp", None, "tensor"),
        P("tensor", "dp"),
        P("dp", "tensor"),
        P(),
        P("tensor", "dp"),
        P(),
    )
    return jax.shard_map(local, mesh=mesh, in_specs=in_specs, out_specs=out_specs, check_vma=False)
```

```python
import functools

import jax
import jax.numpy as jnp
from jax import lax
from jax.experimental import pallas as pl
from jax.experimental.pallas import tpu as pltpu
from jax.sharding import PartitionSpec as P

HD = 72
SHORT = 256
EPSILON = 1e-06
LOG2E = 1.4426950408889634
GELU_ROOT = 0.7978845608028654
GELU_CUBE = 0.044715
F32 = jnp.float32
BF16 = jnp.bfloat16
MIB = 1 << 20
LANES = 128
LIMIT = 24
WORK = 1000000000


def dot(left, right, contract):
    return lax.dot_general(left, right, (contract, ((), ())), preferred_element_type=F32)


NN = ((1,), (0,))
NT = ((1,), (1,))
TN = ((0,), (0,))


def call(body, name, out_shape, scalars, arrays, scratch=(), limit=LIMIT):
    vmem = pl.BlockSpec(memory_space=pltpu.VMEM)
    smem = pl.BlockSpec(memory_space=pltpu.SMEM)
    return pl.pallas_call(
        body,
        out_shape=out_shape,
        in_specs=[smem] * len(scalars) + [vmem] * len(arrays),
        out_specs=jax.tree.map(lambda _: vmem, out_shape),
        scratch_shapes=list(scratch),
        compiler_params=pltpu.CompilerParams(vmem_limit_bytes=limit * MIB),
        cost_estimate=pl.CostEstimate(flops=WORK, bytes_accessed=0, transcendentals=0),
        name=name,
    )(*scalars, *arrays)


def shaped(shape, dtype):
    return jax.ShapeDtypeStruct(tuple(shape), dtype)


def normalize(value):
    center = value - jnp.mean(value, axis=-1, keepdims=True)
    variance = jnp.mean(center * center, axis=-1, keepdims=True)
    inv_std = lax.rsqrt(variance + EPSILON)
    return center * inv_std, inv_std


def norm_back(normed, inv_std, grad_in):
    mean_grad = jnp.mean(grad_in, axis=-1, keepdims=True)
    mean_proj = jnp.mean(grad_in * normed, axis=-1, keepdims=True)
    return inv_std * (grad_in - mean_grad - normed * mean_proj)


def items_body(segments, flags, null_embed, ada, out):
    slots = ada.shape[0]
    for s in range(out.shape[0]):
        item = jnp.minimum(segments[s], slots - 1)
        inside = (segments[s] < slots).astype(F32)
        out[s] = (ada[item] + flags[item].astype(F32) * null_embed[...]) * inside


def qkv_body(index, x, modulation, weight, input_a, out):
    normed, _ = normalize(x[...].astype(F32))
    rows = modulation[index]
    low = (normed * (1.0 + rows[1:2]) + rows[0:1]).astype(BF16)
    input_a[...] = low
    value = dot(low, weight[...], NN).astype(BF16)
    for i in range(value.shape[1] // HD):
        out[:, i * LANES : i * LANES + HD] = value[:, i * HD : (i + 1) * HD]


def chosen(begin, count, size):
    row = lax.broadcasted_iota(jnp.int32, (count, size), 0) + begin
    return (lax.broadcasted_iota(jnp.int32, (count, size), 1) == row).astype(BF16)


def prepare_body(part, folds, where, b_fc1, w_out, wo_part):
    size, cols = wo_part.shape[0], w_out.shape[0]
    out_cols = size * folds
    value = dot(chosen(where[0] * out_cols, out_cols, w_out.shape[1]), w_out[...], NT).astype(BF16)
    for f in range(folds):
        wo_part[:, f * cols : (f + 1) * cols] = value[f * size : (f + 1) * size]
    bias = jnp.broadcast_to(b_fc1[...], (size, b_fc1.shape[1]))
    units = chosen(where[0] * part, part, b_fc1.shape[1])
    wo_part[:, folds * cols : folds * cols + part] = dot(bias, units, NT).astype(BF16)


def pack_body(part, where, w_fc1, w_fc2, first, second):
    units = chosen(where[0] * part, part, w_fc2.shape[0])
    first[...] = dot(units, w_fc1[...], NT).astype(BF16)
    if part % 16 == 0:
        second[...] = w_fc2[pl.ds(pl.multiple_of(where[0] * part, 16), part), :]
    else:
        second[...] = dot(units, w_fc2[...], NN).astype(BF16)


def lay_body(folds, part, *refs):
    given, (out, biases) = refs[:-2], refs[-2:]
    size, count = given[0].shape[0], len(given)
    cols = out.shape[1] // count
    for s, ref in enumerate(given):
        at = (count - s) % count * cols
        for f in range(folds):
            out[f * size : (f + 1) * size, at : at + cols] = ref[:, f * cols : (f + 1) * cols]
        biases[s] = ref[:1, folds * cols : folds * cols + part].astype(F32)


def column(row):
    size = row.shape[1]
    same = lax.broadcasted_iota(jnp.int32, (size, size), 0) == lax.broadcasted_iota(jnp.int32, (size, size), 1)
    return jnp.sum(jnp.where(same, row, 0.0), axis=1, keepdims=True)


def load_body(cotangent, modulation, keep, logit, chan, payload, router):
    rows = cotangent.shape[0]
    routed = column(keep[...] * jax.nn.sigmoid(logit[...]))
    router[...] = routed
    payload[:rows] = (cotangent[...].astype(F32) * modulation[0, 5:6] * routed).astype(BF16)
    payload[rows:] = jnp.zeros((16, payload.shape[1]), BF16)
    payload[rows:, : chan.shape[1]] = jnp.broadcast_to(chan[...], (16, chan.shape[1])).astype(BF16)


def stack_body(*refs):
    begin = 0
    for ref in refs[:-1]:
        refs[-1][begin : begin + ref.shape[0]] = ref[...]
        begin += ref.shape[0]


def rows_of(refs, begin, end):
    found, at = [], 0
    for ref in refs:
        size = ref.shape[0]
        low, high = max(begin - at, 0), min(end - at, size)
        if low < high:
            found.append(ref[low:high])
        at += size
    return jnp.concatenate(found, axis=0) if len(found) > 1 else found[0]


def blocks_of(refs, rows):
    own, from_x, from_y, upper, lower, core = refs
    evens = [[own], [from_x], [from_y], [upper, lower]]
    return [b for i in range(4) for b in (evens[i], [core.at[i * rows : (i + 1) * rows]])]


def flags_body(part, per_quarter, quarters, order, first_group, *refs):
    masks = refs[-1]
    blocks = blocks_of(refs[:-1], refs[0].shape[0])
    units = masks.shape[1]
    quarter = lax.broadcasted_iota(jnp.int32, (1, units), 1) // part
    group = jnp.zeros((1, units), jnp.int32)
    for q in range(quarters):
        group = jnp.where(quarter == q, order[q] * per_quarter + first_group[0], group)
    groups = quarters * per_quarter
    spread = (lax.broadcasted_iota(jnp.int32, (groups, units), 0) == group).astype(BF16)
    end = refs[0].shape[0]
    for m, block in enumerate(blocks):
        chan = rows_of(block, end - 16, end)[:, :groups]
        masks[m : m + 1, :] = dot(chan, spread, NN)[:1]


def place_body(where, *refs):
    weights = refs[-1]
    quarters, width, cols = weights.shape
    out_cols = refs[0].shape[0]
    for m, block in enumerate(blocks_of(refs[:-1], out_cols)):
        at = pl.multiple_of(where[m] * out_cols, 16)
        rows = rows_of(block, 0, out_cols)
        for i in range(quarters):
            weights[i, pl.ds(at, out_cols), :] = rows[:, i * cols : (i + 1) * cols]


def head_of(refs, i):
    return join([r.at[:, i * LANES : i * LANES + HD] for r in refs])


def attend_body(rows, heads, order, segs, head_on, *refs):
    blocks = len(refs) - 1
    qkv, out = refs[:blocks], refs[blocks]
    cols = heads * HD
    scale = HD**-0.5 * LOG2E
    bias = jnp.concatenate(
        [jnp.full((1, rows), jnp.where(segs[j] == segs[order], 0.0, -1e30), F32) for j in range(blocks)], axis=1
    )
    folds = out.shape[1] // cols
    fold_rows = rows // folds
    for h in range(heads):
        q = head_of([qkv[order]], h)
        k = head_of(qkv, heads + h)
        v = head_of(qkv, 2 * heads + h)
        scores = dot(q, k, NT) * scale + bias
        powered = jnp.exp2(scores - jnp.max(scores, axis=1, keepdims=True))
        total = jnp.sum(powered, axis=1, keepdims=True)
        mixed = dot(powered.astype(BF16), v, NN) * (head_on[order, h] / total)
        mixed = mixed.astype(BF16)
        for f in range(folds):
            out[:, f * cols + h * HD : f * cols + (h + 1) * HD] = mixed[f * fold_rows : (f + 1) * fold_rows]


def unfold(ref, cols):
    folds = ref.shape[1] // cols
    return jnp.concatenate([ref[:, f * cols : (f + 1) * cols] for f in range(folds)], axis=0)


def project_body(cols, tokens, modulation, weight, *refs):
    pieces, (attn_out, middle, input_m) = refs[:-3], refs[-3:]
    rows = modulation[0]
    total = 0.0
    for s, piece in enumerate(pieces):
        total = total + dot(unfold(piece, cols), weight[s], NT)
    attn_out[...] = total
    value = tokens[...].astype(F32) + rows[2:3] * total
    middle[...] = value
    normed, _ = normalize(value)
    input_m[...] = (normed * (1.0 + rows[4:5]) + rows[3:4]).astype(BF16)


def join(refs):
    return jnp.concatenate([r[...] for r in refs], axis=0) if len(refs) > 1 else refs[0][...]


def mlp_body(sizes, quarters, part, picks, masks, bias, *refs):
    w1, w2 = join(refs[:quarters]), join(refs[quarters : 2 * quarters])
    refs = refs[2 * quarters :]
    count = sum(sizes)
    xs, refs = refs[:count], refs[count:]
    outs = refs[-2 - len(sizes) : -2]
    hidden_ref, grad_ref = refs[-2:]
    rows = outs[0].shape[0]
    givens = refs[: -2 - len(sizes)]
    givens = [[g] for g in givens] if len(givens) == 1 else blocks_of(givens, givens[0].shape[0])
    bias = jnp.concatenate([bias[q] for q in range(quarters)], axis=1)
    begin = 0
    for b, size in enumerate(sizes):
        x, g = join(xs[begin : begin + size]), rows_of(givens[picks[b]], 0, rows)
        begin += size
        mask = masks[picks[b] : picks[b] + 1, :]
        v = dot(x, w1, NT) + bias
        grad_hidden = dot(g, w2, NT)
        square = v * v
        t = jnp.tanh(GELU_ROOT * v * (1.0 + GELU_CUBE * square))
        half = 0.5 * (1.0 + t)
        slope = half + 0.5 * v * (1.0 - t * t) * (GELU_ROOT * (1.0 + 3.0 * GELU_CUBE * square))
        hidden_ref[b * rows : (b + 1) * rows, :] = (v * half * mask).astype(BF16)
        grad_pre = (grad_hidden * mask * slope).astype(BF16)
        grad_ref[b * rows : (b + 1) * rows, :] = grad_pre
        outs[b][...] = dot(grad_pre, w1, NN).astype(BF16)


def branch_body(quarters, count, *refs):
    w2, refs = join(refs[:quarters]), refs[quarters:]
    hiddens, (keep, send) = refs[:count], refs[count:]
    rows = keep.shape[1]
    b = 0
    for hidden in hiddens:
        for i in range(hidden.shape[0] // rows):
            (send if b % 2 else keep)[b // 2] = dot(hidden[i * rows : (i + 1) * rows, :], w2, NN).astype(BF16)
            b += 1


def split_rows(where, total, keep, send):
    size = keep.shape[1]
    for m in range(2 * keep.shape[0]):
        at = pl.multiple_of(where[m] * size, 16)
        (send if m % 2 else keep)[m // 2] = total[pl.ds(at, size), :].astype(BF16)


def fold_body(cut, count, whole, *refs):
    outs = list(refs[2 * count :])
    for i in range(count):
        total = (refs[i][...].astype(F32) + refs[count + i][...].astype(F32)).astype(BF16)
        if i < whole:
            outs.pop(0)[...] = total
        else:
            outs.pop(0)[...] = total[:cut]
            outs.pop(0)[...] = total[cut:]


def fc_grad_body(count, split, rows, order, *refs):
    acts, given, out, sums = refs[:count], refs[count:-2], refs[-2], refs[-1]
    if split:
        blocks = [rows_of(b, 0, rows) for b in blocks_of(given, given[0].shape[0])]
    else:
        blocks = [ref[...] for ref in given]
    given = jnp.concatenate(blocks, axis=0)
    acc, total, begin = 0.0, 0.0, 0
    for act in acts:
        size = act.shape[0]
        acc = acc + dot(act[...], given[begin : begin + size], TN)
        total = total + jnp.sum(act[...].astype(F32), axis=0, keepdims=True)
        begin += size
    sums[...] = total
    quarters = order.shape[0]
    part = out.shape[0] // quarters
    for s in range(quarters):
        out[pl.ds(pl.multiple_of(order[s] * part, 16), part), :] = acc[s * part : (s + 1) * part].astype(BF16)


def fc_turn_body(first, second, out):
    part, size = first.shape[0], out.shape[1]
    for i, total in enumerate((first, second)):
        for d in range(out.shape[0]):
            out[d, :, i * part : (i + 1) * part] = total[:, d * size : (d + 1) * size].T


def fc_leave_body(given, first, second):
    part = given.shape[2] // 2
    for d in range(given.shape[0]):
        first[:, d * part : (d + 1) * part] = given[d, :, :part].astype(F32)
        second[:, d * part : (d + 1) * part] = given[d, :, part:].astype(F32)


def total_of(begins, takes, refs):
    whole = refs[0][...].astype(F32)
    rows = whole.shape[0]
    for begin, take, ref in zip(begins[1:], takes[1:], refs[1:]):
        take = ref.shape[0] if take is None else take
        piece = ref[:take].astype(F32)
        if take < rows:
            blank = [jnp.zeros((n, piece.shape[1]), F32) for n in (begin, rows - begin - take)]
            piece = jnp.concatenate([b for b in (blank[0], piece, blank[1]) if b.shape[0]], axis=0)
        whole = whole + piece
    return whole


def middle_back_body(cols, begins, cotangent, modulation, middle, attn_out, weight, *refs):
    count = len(begins)
    grad_middle, grad_attn, sums = refs[count : count + 3]
    pieces = refs[count + 3 :]
    grad_in = total_of(begins, [None] * count, refs[:count])
    rows = modulation[0]
    normed, inv_std = normalize(middle[...])
    grad = cotangent[...].astype(F32) + norm_back(normed, inv_std, grad_in * (1.0 + rows[4:5]))
    grad_middle[...] = grad
    sums[0:1] = jnp.sum(grad * attn_out[...], axis=0, keepdims=True)
    sums[1:2] = jnp.sum(grad_in, axis=0, keepdims=True)
    sums[2:3] = jnp.sum(grad_in * normed, axis=0, keepdims=True)
    low = (grad * rows[2:3]).astype(BF16)
    grad_attn[...] = low
    folds = pieces[0].shape[1] // cols
    fold_rows = low.shape[0] // folds
    for s, piece in enumerate(pieces):
        value = dot(low, weight[s], NN).astype(BF16)
        for f in range(folds):
            piece[:, f * cols : (f + 1) * cols] = value[f * fold_rows : (f + 1) * fold_rows]


def attend_back_body(rows, heads, segs, head_on, *refs):
    blocks = (len(refs) - 2) // 3
    qkv, grads, outs = refs[:blocks], refs[blocks : 2 * blocks], refs[2 * blocks : 3 * blocks]
    dk_ref, dv_ref = refs[3 * blocks :]
    cols = heads * HD
    scale = HD**-0.5 * LOG2E
    given = [unfold(g, cols) for g in grads]
    for i in range(blocks):
        bias = jnp.concatenate(
            [jnp.full((rows, 1), jnp.where(segs[j] == segs[i], 0.0, -1e30), F32) for j in range(blocks)], axis=0
        )
        for h in range(heads):
            q = head_of([qkv[i]], h)
            k = head_of(qkv, heads + h)
            v = head_of(qkv, 2 * heads + h)
            g = (given[i][:, h * HD : (h + 1) * HD].astype(F32) * head_on[i, h]).astype(BF16)
            scores = dot(k, q, NT) * scale + bias
            powered = jnp.exp2(scores - jnp.max(scores, axis=0, keepdims=True))
            prob = powered * (1.0 / jnp.sum(powered, axis=0, keepdims=True))
            grad_prob = dot(v, g, NT)
            inner = jnp.sum(prob * grad_prob, axis=0, keepdims=True)
            grad_score = (prob * (grad_prob - inner)).astype(BF16)
            dv = dot(prob.astype(BF16), g, NN)
            dk = dot(grad_score, q, NN)
            dq = dot(grad_score, k, TN)
            outs[i][:, h * HD : (h + 1) * HD] = (dq * HD**-0.5).astype(BF16)
            dk_ref[h] = dk if i == 0 else dk_ref[h] + dk
            dv_ref[h] = dv if i == 0 else dv_ref[h] + dv
    for h in range(heads):
        for i in range(blocks):
            dk = dk_ref[h, i * rows : (i + 1) * rows, :] * HD**-0.5
            dv = dv_ref[h, i * rows : (i + 1) * rows, :]
            outs[i][:, cols + h * HD : cols + (h + 1) * HD] = dk.astype(BF16)
            outs[i][:, 2 * cols + h * HD : 2 * cols + (h + 1) * HD] = dv.astype(BF16)


def qkv_grads_body(blocks, *refs):
    xs, gs = refs[:blocks], refs[blocks : 2 * blocks]
    acc = 0.0
    for x, g in zip(xs, gs):
        acc = acc + dot(x[...], g[...], TN)
    refs[-1][...] = acc.astype(BF16)


def out_grads_body(cols, blocks, where, grad, *refs):
    outs, total = refs[blocks:-1], refs[-1]
    for s, piece in enumerate(refs[:blocks]):
        total[:, s * cols : (s + 1) * cols] = dot(grad[...], unfold(piece, cols), TN)
    if len(outs) == 1:
        outs[0][...] = total[...].astype(BF16)
        return
    split_rows(where, total, *outs)


def fold_b_body(cut, x, x_got, y, y_got, via_x, via_y, x_upper, y_lower, last_x, last_y):
    for_x = x[...].astype(F32) + x_got[...].astype(F32)
    for_y = y[...].astype(F32) + y_got[...].astype(F32)
    x_upper[...] = for_x[:cut].astype(BF16)
    last_x[...] = (for_x[cut:] + via_y[...].astype(F32)).astype(BF16)
    last_y[...] = (for_y[:cut] + via_x[...].astype(F32)).astype(BF16)
    y_lower[...] = for_y[cut:].astype(BF16)


def fold_near_body(cut, keep, got, own, for_x, for_y, send_x, send_y):
    rows = own.shape[0]
    blocks = [(keep[i].astype(F32) + got[i].astype(F32)).astype(BF16) for i in range(4)]
    own[...] = blocks[0]
    for_x[...] = blocks[1][cut:]
    for_y[...] = blocks[2][:cut]
    send_x[:cut] = blocks[1][:cut]
    send_x[cut:] = blocks[3][:cut]
    send_y[: rows - cut] = blocks[2][cut:]
    send_y[rows - cut :] = blocks[3][cut:]


def add_body(*refs):
    count = len(refs) // 3
    for a, b, out in zip(refs[:count], refs[count : 2 * count], refs[2 * count :]):
        out[...] = (a[...].astype(F32) + b[...].astype(F32)).astype(BF16)


def far_body(count, *refs):
    for i in range(count):
        for_x, for_y, got_x, got_y = refs[4 * i : 4 * i + 4]
        last_x, last_y = refs[4 * count + 2 * i : 4 * count + 2 * i + 2]
        cut, rest = for_y.shape[0], for_x.shape[0]
        last_x[...] = (for_x[...].astype(F32) + got_y[rest:].astype(F32)).astype(BF16)
        last_y[...] = (for_y[...].astype(F32) + got_x[cut:].astype(F32)).astype(BF16)


def parts_body(count, weight, *refs):
    for g, out in zip(refs[:count], refs[count:]):
        out[...] = dot(g[...], weight[...], NT).astype(BF16)


def out_sum_body(begins, takes, *refs):
    total = total_of(begins, takes, refs[: len(begins)])
    pieces = refs[len(begins) :]
    cols = pieces[0].shape[1]
    for s, piece in enumerate(pieces):
        piece[...] = total[:, s * cols : (s + 1) * cols].astype(BF16)


def qkv_leave_body(given, out):
    cols = out.shape[2]
    for i in range(3):
        out[:, i, :] = given[:, i * cols : (i + 1) * cols].astype(F32)


def leave_body(begins, takes, cotangent, router, modulation, middle, *refs):
    count = len(begins)
    output, sums = refs[count:]
    routed = router[...] * total_of(begins, takes, refs[:count])
    output[...] = (middle[...] + modulation[0, 5:6] * routed).astype(BF16)
    sums[...] = jnp.sum(cotangent[...].astype(F32) * routed, axis=0, keepdims=True)


def null_body(flags, *refs):
    count = (len(refs) - 1) // 2
    xs, parts, out = refs[:count], refs[count : 2 * count], refs[-1]
    first, second = 0.0, 0.0
    for s in range(count):
        normed, _ = normalize(xs[s][...].astype(F32))
        grad = parts[s][...].astype(F32) * flags[s]
        first = first + jnp.sum(grad, axis=0, keepdims=True)
        second = second + jnp.sum(grad * normed, axis=0, keepdims=True)
    out[0:1] = first
    out[1:2] = second


def token_back_body(tokens, modulation, grad_middle, own, received, grad_tokens):
    normed, inv_std = normalize(tokens[...].astype(F32))
    grad_in = own[...].astype(F32) + received[...].astype(F32)
    grad = grad_middle[...] + norm_back(normed, inv_std, grad_in * (1.0 + modulation[0, 1:2]))
    grad_tokens[...] = grad.astype(BF16)


def after(value, *others):
    return lax.optimization_barrier((value, others))[0]


def together(*values):
    return lax.optimization_barrier(values)


def shift(value, axis, size, step):
    return lax.ppermute(value, axis, [(i, (i + step) % size) for i in range(size)])


def swap(value, axis, size, bit):
    return lax.ppermute(value, axis, [(i, i ^ bit) for i in range(size)])


def ring_gather(block, axis, size):
    blocks = [block]
    for _ in range(size - 1):
        blocks.append(shift(blocks[-1], axis, size, 1))
    return blocks


def ring_reduce(parts, axis, size):
    total = parts[1 % size]
    for step in range(2, size + 1):
        total = shift(total, axis, size, 1)
        if step < size:
            total = total + parts[step]
    return parts[0], total


def cube_gather(block, axis, size):
    block = block[None]
    bit = 1
    while bit < size:
        block = jnp.concatenate([block, swap(block, axis, size, bit)], axis=0)
        bit *= 2
    return block


def cube_sum(value, axis, size):
    bit = 1
    while bit < size:
        value = value + swap(value, axis, size, bit)
        bit *= 2
    return value


def shift_all(parts, axis, size, sign):
    return [parts[0]] + [shift(parts[s], axis, size, sign * s) for s in range(1, size)]


def far(from_x, from_y, cut):
    return [swap(from_y[:cut], "dp", 8, 2), swap(from_x[cut:], "dp", 8, 4)]


def with_core(name, blocks):
    rows = sum(b.shape[0] for b in blocks)
    stacked = call(stack_body, name, shaped((rows, blocks[0].shape[1]), BF16), [], blocks)
    return [*blocks, swap(stacked, "dp", 8, 1)]


def add(name, *pairs):
    return call(
        add_body, name, tuple(shaped(a.shape, BF16) for a, _ in pairs), [], [a for a, _ in pairs] + [b for _, b in pairs]
    )


def fold(name, pairs, cut):
    rows, cols = pairs[0][0].shape
    return call(
        functools.partial(fold_body, cut, len(pairs), 0),
        name,
        tuple([shaped((cut, cols), BF16), shaped((rows - cut, cols), BF16)] * len(pairs)),
        [],
        [a for a, _ in pairs] + [b for _, b in pairs],
    )


def reduce_near(name, keep, got, cut):
    _, rows, cols = keep.shape
    sizes = (rows, rows - cut, cut, 2 * cut, 2 * (rows - cut))
    own, for_x, for_y, send_x, send_y = call(
        functools.partial(fold_near_body, cut),
        name,
        tuple(shaped((n, cols), BF16) for n in sizes),
        [],
        [keep, got],
    )
    return [own, for_x, for_y, swap(send_x, "dp", 8, 2), swap(send_y, "dp", 8, 4)]


def reduce_far(name, *states):
    shapes = [shaped(a.shape, BF16) for state in states for a in state[1:3]]
    marks = call(functools.partial(far_body, len(states)), name, tuple(shapes), [], [a for st in states for a in st[1:]])
    found = []
    for i, (own, for_x, for_y, got_x, got_y) in enumerate(states):
        cut, rest = for_y.shape[0], for_x.shape[0]
        last_x, last_y = swap(marks[2 * i], "dp", 8, 2), swap(marks[2 * i + 1], "dp", 8, 4)
        found.append(([0, 0, cut, 0, cut], [None, cut, None, None, rest], [own, got_x, last_x, last_y, got_y]))
    return *found, marks


def local(
    tokens,
    w_qkv,
    w_out,
    w_fc1,
    b_fc1,
    w_fc2,
    null_embed,
    ada_embed,
    item_len,
    null_flag,
    head_mask,
    group_mask,
    token_keep,
    router_logit,
    cotangent,
):
    n_tensor = lax.axis_size("tensor")
    n_dp = lax.axis_size("dp")
    z = lax.axis_index("tensor")
    p = lax.axis_index("dp")
    rows, width = tokens.shape
    group_rows = rows * n_tensor
    local_cols = w_qkv.shape[2]
    local_heads = local_cols // HD
    local_hidden = w_fc1.shape[1]
    part = local_hidden // n_dp
    hidden_units = part * n_tensor
    out_cols = width // n_dp
    slots = item_len.shape[1]
    chan_size = local_hidden * n_tensor // group_mask.shape[2]
    local_groups = group_mask.shape[2] // n_tensor
    folds = 4
    assert SHORT % rows == 0 and chan_size % part == 0 and n_dp & (n_dp - 1) == 0
    piece_shape = shaped((rows // folds, folds * local_cols), BF16)
    block_shape = shaped((rows, width), BF16)

    cube = n_dp == 8 and n_tensor == 4
    payload_rows = rows + 16
    cut = payload_rows // 2 // 16 * 16
    half = rows // 2
    out_cut = out_cols // 2 // 16 * 16
    lengths, flags = item_len[0], null_flag[0]

    rows_x = [tokens, shift(tokens, "tensor", n_tensor, 1)]
    mine_index = p[None].astype(jnp.int32)
    peers = (p ^ jnp.arange(n_dp)).astype(jnp.int32)
    order = ((z - jnp.arange(n_tensor)) % n_tensor).astype(jnp.int32)
    first_group = (p * part // chan_size)[None].astype(jnp.int32)
    wo_folds = 3 if out_cols % 48 == 0 else 1
    wo_lanes = -(-(wo_folds * local_cols + part) // LANES) * LANES
    wo_part = call(
        functools.partial(prepare_body, part, wo_folds),
        "prepare",
        shaped((out_cols // wo_folds, wo_lanes), BF16),
        [mine_index],
        [b_fc1[None], w_out],
    )
    wo_mine = [wo_part, shift(wo_part, "tensor", n_tensor, 1)]

    starts = order * rows
    ends = jnp.sum(jnp.where(jnp.arange(slots)[:, None] >= jnp.arange(slots)[None, :], lengths[None, :], 0), axis=1)
    segments = jnp.sum((ends[None, :] <= starts[:, None]).astype(jnp.int32), axis=1)
    hot = (segments[:, None] == jnp.arange(slots)[None, :]).astype(F32)
    heads_here = lax.dynamic_slice_in_dim(head_mask[0], z * local_heads, local_heads, 1).astype(F32)
    head_on = jnp.sum(hot[:, :, None] * heads_here[None], axis=1)
    nulls = jnp.sum(hot * flags.astype(F32)[None], axis=1)
    my_chan = jnp.sum(hot[0][:, None] * group_mask[0].astype(F32), axis=0)[None]
    modulation = call(
        items_body,
        "items",
        shaped((n_tensor, 6, width), F32),
        [segments, flags],
        [null_embed, ada_embed[0]],
    )
    payload, router = call(
        load_body,
        "load",
        (shaped((payload_rows, width), BF16), shaped((rows, 1), F32)),
        [],
        [cotangent, modulation, token_keep.astype(F32)[None], router_logit[None], my_chan],
    )
    flat_qkv = w_qkv.reshape(width, 3 * local_cols)

    def project_in(s, block):
        return call(
            functools.partial(qkv_body, s),
            f"qkv_{s}",
            (block_shape, shaped((rows, 3 * local_heads * LANES), BF16)),
            [],
            [block, modulation, flat_qkv],
        )

    rows_x[1], wo_mine[1], payload = together(rows_x[1], wo_mine[1], payload)
    if cube:
        pay_x, pay_y = swap(payload, "dp", n_dp, 2), swap(payload, "dp", n_dp, 4)
    rows_x.append(shift(rows_x[1], "tensor", n_tensor, 1))
    wo_mine.append(shift(wo_mine[1], "tensor", n_tensor, 1))
    w1_part, w2_part = call(
        functools.partial(pack_body, part),
        "pack",
        (shaped((part, width), BF16),) * 2,
        [after(mine_index, payload)],
        [w_fc1, w_fc2],
    )
    input_a, qkv = zip(project_in(0, after(rows_x[0], rows_x[1])), project_in(1, rows_x[1]))
    input_a, qkv = [*input_a], [*qkv]
    rows_x[2], wo_mine[2], w1_part, qkv = together(rows_x[2], wo_mine[2], w1_part, qkv)
    for s in range(2, n_tensor):
        if s + 1 < n_tensor:
            rows_x.append(shift(rows_x[s], "tensor", n_tensor, 1))
            wo_mine.append(shift(wo_mine[s], "tensor", n_tensor, 1))
        if cube and s == 2:
            pay_x, pay_y = after((pay_x, pay_y), rows_x[2])
            pay_far = far(pay_x, pay_y, cut)
        low, value = project_in(s, rows_x[s])
        input_a.append(low)
        qkv.append(value)
        if cube and s == 2:
            pay_blocks = [payload, pay_x, pay_y, *pay_far]
            pay_stack = call(
                stack_body, "stack_pay", shaped((4 * payload_rows, width), BF16), [], after(pay_blocks, value)
            )
            rows_x[3], wo_mine, value, pay_stack, w1_part = together(rows_x[3], wo_mine, value, pay_stack, w1_part)
            qkv[2] = value
        elif s + 1 < n_tensor:
            rows_x[s + 1] = after(rows_x[s + 1], value)
    w1 = [w1_part, shift(after(w1_part, rows_x[-1]), "tensor", n_tensor, 1)]
    wo_flat, biases = call(
        functools.partial(lay_body, wo_folds, part),
        "lay",
        (shaped((out_cols, n_tensor * local_cols), BF16), shaped((n_tensor, 1, part), F32)),
        [],
        wo_mine,
    )
    if cube:
        pay_core = swap(pay_stack, "dp", n_dp, 1)
        wo_x, wo_y = swap(wo_flat, "dp", n_dp, 2), swap(wo_flat, "dp", n_dp, 4)

    def attend(s, qkv):
        return call(
            functools.partial(attend_body, rows, local_heads, s),
            f"attend_{s}",
            piece_shape,
            [segments, head_on],
            [*qkv],
        )

    pieces, mine = {}, {}
    away = [n_tensor // 2] + [s for s in range(1, n_tensor) if s != n_tensor // 2]
    for step, s in enumerate([*away, 0]):
        pieces[s] = attend(s, qkv)
        qkv = after(qkv, pieces[s])
        if step == 1 and cube:
            pieces, w1[1], wo_x, wo_y, pay_core, qkv = together(pieces, w1[1], wo_x, wo_y, pay_core, qkv)
            w1.append(shift(w1[1], "tensor", n_tensor, 1))
            wo_far = far(wo_x, wo_y, out_cut)
    if cube:
        sent = {s: shift(pieces[s], "tensor", n_tensor, -s) for s in away[:2]}
        wo_blocks = [wo_flat, wo_x, wo_y, *wo_far]
        pieces, w1[2], wo_far, wo_stack = together(
            pieces, w1[2], wo_far, call(stack_body, "stack_wo", shaped((4 * out_cols, width), BF16), [], wo_blocks)
        )
        wo_core = swap(wo_stack, "dp", n_dp, 1)
        w1.append(shift(w1[2], "tensor", n_tensor, 1))
        wo_all = call(
            place_body,
            "place",
            shaped((n_tensor, width, local_cols), BF16),
            [peers],
            [wo_flat, wo_x, wo_y, *wo_far, wo_core],
        )
        payloads = [payload, pay_x, pay_y, *pay_far, pay_core]
        masks = call(
            functools.partial(flags_body, part, local_groups, n_tensor),
            "flags",
            shaped((n_dp, hidden_units), F32),
            [order, first_group],
            after(payloads, pieces[0]),
        )
        mine = [pieces[0] if s == 0 else sent[s] if s in sent else shift(pieces[s], "tensor", n_tensor, -s) for s in range(n_tensor)]
        mine, wo_all, masks = together(mine, wo_all, masks)
    else:
        mine = shift_all([pieces[s] for s in range(n_tensor)], "tensor", n_tensor, -1)
        wo_all = lax.all_gather(wo_flat, "dp", axis=0).reshape(n_dp, out_cols, n_tensor, local_cols)
        wo_all = wo_all.transpose(2, 0, 1, 3).reshape(n_tensor, width, local_cols)
        payloads = lax.all_gather(payload, "dp", axis=0)
        chan = payloads[:, rows, : n_tensor * local_groups].astype(F32)
        chan = chan.reshape(n_dp, n_tensor, local_groups)
        chan = lax.dynamic_index_in_dim(chan, first_group[0], 2, False)[:, order]
        masks = jnp.repeat(chan, part, axis=1)
        while len(w1) < n_tensor:
            w1.append(shift(w1[-1], "tensor", n_tensor, 1))
        w2 = ring_gather(w2_part, "tensor", n_tensor)
    attn_out, middle, input_m = call(
        functools.partial(project_body, local_cols),
        "project",
        (shaped((rows, width), F32), shaped((rows, width), F32), block_shape),
        [],
        [tokens, modulation, wo_all, *mine],
    )

    def mlp(name, picks, masks, xs, gs):
        acts = shaped((len(xs) * rows, hidden_units), BF16)
        return call(
            functools.partial(mlp_body, [len(x) for x in xs], n_tensor, part, picks),
            name,
            (*[block_shape] * len(xs), acts, acts),
            [],
            [masks, biases, *w1, *w2, *sum(xs, []), *gs],
        )

    def fc_grad(name, acts, arrays, split):
        return call(
            functools.partial(fc_grad_body, len(acts), split, rows),
            name,
            (shaped((hidden_units, width), BF16), shaped((1, hidden_units), F32)),
            [order],
            [*acts, *arrays],
        )

    if cube:
        core, from_x, from_y = [swap(input_m, "dp", n_dp, bit) for bit in (1, 2, 4)]
        w2 = [w2_part, shift(after(w2_part, w1[3]), "tensor", n_tensor, 1)]
        core, from_x, from_y, w2[1] = together(core, from_x, from_y, w2[1])
        w2.append(shift(w2[1], "tensor", n_tensor, 1))
        upper, lower = far(from_x, from_y, half)
        from_xc, from_yc = swap(from_x, "dp", n_dp, 1), swap(from_y, "dp", n_dp, 1)
        near_x, upper, lower, w2[2] = together([from_x, from_xc, from_y, from_yc], upper, lower, w2[2])
        w2.append(shift(w2[2], "tensor", n_tensor, 1))
        upper_c, lower_c = swap(upper, "dp", n_dp, 1), swap(lower, "dp", n_dp, 1)
        far_x = [upper, lower, upper_c, lower_c]
        w2[3], far_x = together(w2[3], far_x)
        *part_c, hidden_c, pre_c = mlp("mlp_6", (6, 7), masks, [far_x[:2], far_x[2:]], payloads)
        cross = fold("fold_c", [(part_c[0], swap(part_c[1], "dp", n_dp, 1))], half)
        near_x, cross = together(near_x, cross)
        via_x, via_y = swap(cross[0], "dp", n_dp, 2), swap(cross[1], "dp", n_dp, 4)
        *part_b, hidden_b, pre_b = mlp("mlp_2", (2, 3, 4, 5), masks, [[b] for b in near_x], payloads)
        part_b, via_x, via_y = together(part_b, via_x, via_y)
        part_b = [(part_b[m], swap(part_b[m + 1], "dp", n_dp, 1)) for m in (0, 2)]
        x_upper, y_lower, last_x, last_y = call(
            functools.partial(fold_b_body, half),
            "fold_b",
            (shaped((half, width), BF16),) * 4,
            [],
            [*part_b[0], *part_b[1], via_x, via_y],
        )
        first_x, x_upper, y_lower, last_x, last_y = together([input_m, core], x_upper, y_lower, last_x, last_y)
        x_upper, y_lower = swap(x_upper, "dp", n_dp, 2), swap(y_lower, "dp", n_dp, 4)
        x_lower, y_upper = swap(last_x, "dp", n_dp, 2), swap(last_y, "dp", n_dp, 4)
        *part_a, hidden_a, pre_a = mlp("mlp_0", (0, 1), masks, [[b] for b in first_x], payloads)
        hiddens, grad_pres = [hidden_a, hidden_b, hidden_c], [pre_a, pre_b, pre_c]
        rows_m = [*first_x, *near_x, *far_x]
        grad_fc2, _ = fc_grad("fc2_grad", hiddens, payloads, True)
        own = [part_a[0], swap(part_a[1], "dp", n_dp, 1)]
        branch_keep, branch_send = call(
            functools.partial(branch_body, n_tensor, len(hiddens)),
            "branch",
            tuple([shaped((n_dp // 2, rows, width), BF16)] * 2),
            [],
            [*w2, *after(hiddens, grad_fc2)],
        )
        grad_in_m = [*own, x_upper, x_lower, y_upper, y_lower]
        begins = [0, 0, 0, half, 0, half]
        grad_in_m, branch_keep, branch_send = together(grad_in_m, branch_keep, branch_send)
    else:
        rows_m = lax.all_gather(input_m, "dp", axis=0)

        def step(sums, given):
            x, g, m = given
            out, hidden, grad_pre = mlp("mlp", (0,), m[None], [[x]], [g])
            sums = [a + dot(b, c, TN) for a, b, c in zip(sums, (grad_pre, hidden), (x, g[:rows]))]
            return sums, (out, hidden, jnp.sum(grad_pre.astype(F32), axis=0, keepdims=True))

        zero = jnp.zeros((hidden_units, width), F32)
        sums, (grad_parts, hidden, grad_bias) = lax.scan(step, [zero, zero], (rows_m, payloads, masks))
        begins, grad_in_m = [0], [lax.psum_scatter(grad_parts, "dp", scatter_dimension=0)]
        grad_bias = jnp.sum(grad_bias, axis=0)
        sums = [a.astype(BF16).reshape(n_tensor, part, width) for a in sums]
        grad_fc1, grad_fc2 = [jnp.take(a, order, axis=0).reshape(hidden_units, width) for a in sums]

    def fc_scatter(value):
        return lax.psum_scatter(value.reshape(n_tensor, part, width), "tensor", scatter_dimension=0)

    fc2_sum = fc_scatter(grad_fc2)
    grad_middle, grad_attn, sums_m, *grad_pieces = call(
        functools.partial(middle_back_body, local_cols, begins),
        "middle_back",
        (shaped((rows, width), F32), block_shape, shaped((3, width), F32), *[piece_shape] * n_tensor),
        [],
        [cotangent, modulation, middle, attn_out, wo_all, *grad_in_m],
    )
    grads = shift_all(grad_pieces, "tensor", n_tensor, 1)
    late_attn = after(grad_attn, grad_pieces)

    if cube:
        grad_fc1, grad_bias = fc_grad("fc1_grad", after(grad_pres, late_attn), rows_m, False)
        late_attn = after(late_attn, grad_bias)
    grad_wout = call(
        functools.partial(out_grads_body, local_cols, n_tensor),
        "out_grads",
        (shaped((4, out_cols, width), BF16),) * 2 if cube else (shaped((width, width), BF16),),
        [peers],
        [late_attn, *mine],
        scratch=[pltpu.VMEM((width, width), F32)],
    )
    if cube:
        branch_got = swap(branch_send, "dp", n_dp, 1)
        grads, branch_got, grad_wout, grad_fc1 = together(grads, branch_got, grad_wout, grad_fc1)
        wout_got = swap(grad_wout[1], "dp", n_dp, 1)
        branch_state = reduce_near("branch_near", branch_keep, branch_got, half)
        grads = after(grads, branch_state[0])
    else:
        w2 = jnp.concatenate(w2, axis=0)
        branch = after(hidden, grad_fc1).reshape(n_dp * rows, hidden_units)
        branch = dot(branch, w2, NN).astype(BF16).reshape(n_dp, rows, width)
        late_begins, takes, branch = [0], [None], [lax.psum_scatter(branch, "dp", scatter_dimension=0)]
        wout_sum = lax.psum_scatter(grad_wout[0].reshape(n_dp, out_cols, width), "dp", scatter_dimension=0)
    fc1_sum = fc_scatter(grad_fc1)

    grad_rows = call(
        functools.partial(attend_back_body, rows, local_heads),
        "attend_back",
        tuple([shaped((rows, 3 * local_cols), BF16)] * n_tensor),
        [segments, head_on],
        [*qkv, *grads],
        scratch=[pltpu.VMEM((local_heads, group_rows, HD), F32)] * 2,
        limit=48,
    )

    def grad_parts_of(name, given):
        return call(
            functools.partial(parts_body, len(given)), name, (block_shape,) * len(given), [], [flat_qkv, *given]
        )

    (first,) = grad_parts_of("part_1", [grad_rows[1]])
    later = after(grad_rows, first)
    if cube:
        first, later, branch_state, wout_got = together(first, later, branch_state, wout_got)
    total = shift(first, "tensor", n_tensor, 1)
    grad_wqkv = call(
        functools.partial(qkv_grads_body, n_tensor),
        "qkv_grads",
        shaped((width, 3 * local_cols), BF16),
        [],
        [*input_a, *later],
    )
    qkv_sum = lax.psum_scatter(grad_wqkv.reshape(n_dp, out_cols, 3 * local_cols), "dp", scatter_dimension=0)
    later = after(later, grad_wqkv)
    if cube:
        (late_begins, takes, branch), branch_marks = reduce_far("branch_far", after(branch_state, grad_wqkv))
        wout_state = reduce_near("wout_near", *after((grad_wout[0], wout_got), branch_marks), out_cut)
        later = after(later, wout_state[0])
    others = [s for s in range(n_tensor) if s != 1]
    grad_in_parts = dict(zip(others, grad_parts_of("parts", [later[s] for s in others])))
    grad_in_parts = [first if s == 1 else grad_in_parts[s] for s in range(n_tensor)]
    sums_a = call(null_body, "null", shaped((2, width), F32), [nulls], [*rows_x, *grad_in_parts])
    if cube:
        total, grad_in_parts, branch, wout_state, sums_a = together(total, grad_in_parts, branch, wout_state, sums_a)
    total = total + grad_in_parts[2 % n_tensor]
    mark = total
    total = shift(total, "tensor", n_tensor, 1)
    if cube:
        (wout_begins, wout_takes, wout_last), wout_marks = reduce_far("wout_far", wout_state)
        branch = after(branch, wout_marks)
    output, sums_b = call(
        functools.partial(leave_body, late_begins, takes),
        "leave",
        (block_shape, shaped((1, width), F32)),
        [],
        [cotangent, router, modulation, middle, *branch],
    )
    bias_full = lax.dynamic_update_slice_in_dim(
        jnp.zeros((n_tensor, local_hidden), F32), grad_bias.reshape(n_tensor, part)[order], p * part, 1
    )
    small = jnp.concatenate(
        [bias_full.reshape(-1, width), sums_a, nulls[0] * sums_m, nulls[0] * sums_b], axis=0
    )
    small = cube_sum(small, "dp", n_dp)
    if cube:
        total, small, wout_last = together(total, small, wout_last)
    for s in range(3, n_tensor):
        total = total + grad_in_parts[s]
        mark = total
        total = shift(total, "tensor", n_tensor, 1)

    small = small + swap(small, "tensor", n_tensor, 1)
    mark = small
    bit = 2
    while bit < n_tensor:
        small = small + swap(small, "tensor", n_tensor, bit)
        bit *= 2
    if cube:
        wout_parts = call(
            functools.partial(out_sum_body, wout_begins, wout_takes),
            "out_sum",
            tuple([shaped((out_cols, local_cols), BF16)] * n_tensor),
            [],
            wout_last,
        )
    else:
        wout_parts = [wout_sum[:, i * local_cols : (i + 1) * local_cols] for i in range(n_tensor)]
    wout_parts = shift_all(wout_parts, "tensor", n_tensor, 1)
    fc_sum = call(
        fc_turn_body,
        "fc_turn",
        shaped((n_dp, out_cols, 2 * part), BF16),
        [],
        after([fc1_sum, fc2_sum], mark),
    )
    fc_sum = lax.all_to_all(fc_sum, "dp", split_axis=0, concat_axis=0)
    qkv_sum = call(
        qkv_leave_body,
        "qkv_leave",
        shaped((out_cols, 3, local_cols), F32),
        [],
        [qkv_sum],
    )
    fc1_sum, fc2_sum = call(
        fc_leave_body,
        "fc_leave",
        (shaped((out_cols, local_hidden), F32), shaped((out_cols, local_hidden), F32)),
        [],
        [fc_sum],
    )
    wout_sum = sum(x.astype(F32) for x in wout_parts).T
    bias_sum, null_sum = small[:-6].reshape(-1), small[-6:]
    grad_tokens = call(
        token_back_body,
        "token_back",
        block_shape,
        [],
        [tokens, modulation, grad_middle, grad_in_parts[0], total],
    )

    return (
        output,
        grad_tokens,
        qkv_sum,
        wout_sum,
        fc1_sum,
        bias_sum,
        fc2_sum.T,
        null_sum,
    )


def solution(mesh):
    in_specs = (
        P(("dp", "tensor"), None),
        P(None, None, "tensor"),
        P("tensor", None),
        P(None, "tensor"),
        P("tensor"),
        P("tensor", None),
        P(),
        P("dp", None, None, None),
        P("dp", None),
        P("dp", None),
        P("dp", None, None),
        P("dp", None, None),
        P(("dp", "tensor")),
        P(("dp", "tensor")),
        P(("dp", "tensor"), None),
    )
    out_specs = (
        P(("dp", "tensor"), None),
        P(("dp", "tensor"), None),
        P("dp", None, "tensor"),
        P("tensor", "dp"),
        P("dp", "tensor"),
        P(),
        P("tensor", "dp"),
        P(),
    )
    return jax.shard_map(local, mesh=mesh, in_specs=in_specs, out_specs=out_specs, check_vma=False)
```

```python
import functools

import jax
import jax.numpy as jnp
from jax import lax
from jax.experimental import pallas as pl
from jax.experimental.pallas import tpu as pltpu
from jax.sharding import PartitionSpec as P

HD = 72
SHORT = 256
EPSILON = 1e-06
LOG2E = 1.4426950408889634
GELU_ROOT = 0.7978845608028654
GELU_CUBE = 0.044715
F32 = jnp.float32
BF16 = jnp.bfloat16
MIB = 1 << 20
LANES = 128
LIMIT = 24
WORK = 1000000000


def dot(left, right, contract):
    return lax.dot_general(left, right, (contract, ((), ())), preferred_element_type=F32)


NN = ((1,), (0,))
NT = ((1,), (1,))
TN = ((0,), (0,))


def call(body, name, out_shape, scalars, arrays, scratch=(), limit=LIMIT):
    vmem = pl.BlockSpec(memory_space=pltpu.VMEM)
    smem = pl.BlockSpec(memory_space=pltpu.SMEM)
    return pl.pallas_call(
        body,
        out_shape=out_shape,
        in_specs=[smem] * len(scalars) + [vmem] * len(arrays),
        out_specs=jax.tree.map(lambda _: vmem, out_shape),
        scratch_shapes=list(scratch),
        compiler_params=pltpu.CompilerParams(vmem_limit_bytes=limit * MIB),
        cost_estimate=pl.CostEstimate(flops=WORK, bytes_accessed=0, transcendentals=0),
        name=name,
    )(*scalars, *arrays)


def shaped(shape, dtype):
    return jax.ShapeDtypeStruct(tuple(shape), dtype)


def normalize(value):
    center = value - jnp.mean(value, axis=-1, keepdims=True)
    variance = jnp.mean(center * center, axis=-1, keepdims=True)
    inv_std = lax.rsqrt(variance + EPSILON)
    return center * inv_std, inv_std


def norm_back(normed, inv_std, grad_in):
    mean_grad = jnp.mean(grad_in, axis=-1, keepdims=True)
    mean_proj = jnp.mean(grad_in * normed, axis=-1, keepdims=True)
    return inv_std * (grad_in - mean_grad - normed * mean_proj)


def items_body(segments, flags, null_embed, ada, out):
    slots = ada.shape[0]
    for s in range(out.shape[0]):
        item = jnp.minimum(segments[s], slots - 1)
        inside = (segments[s] < slots).astype(F32)
        out[s] = (ada[item] + flags[item].astype(F32) * null_embed[...]) * inside


def qkv_body(index, x, modulation, weight, input_a, out):
    normed, _ = normalize(x[...].astype(F32))
    rows = modulation[index]
    low = (normed * (1.0 + rows[1:2]) + rows[0:1]).astype(BF16)
    input_a[...] = low
    value = dot(low, weight[...], NN).astype(BF16)
    for i in range(value.shape[1] // HD):
        out[:, i * LANES : i * LANES + HD] = value[:, i * HD : (i + 1) * HD]


def chosen(begin, count, size):
    row = lax.broadcasted_iota(jnp.int32, (count, size), 0) + begin
    return (lax.broadcasted_iota(jnp.int32, (count, size), 1) == row).astype(BF16)


def prepare_body(part, folds, where, b_fc1, w_out, wo_part):
    size, cols = wo_part.shape[0], w_out.shape[0]
    out_cols = size * folds
    value = dot(chosen(where[0] * out_cols, out_cols, w_out.shape[1]), w_out[...], NT).astype(BF16)
    for f in range(folds):
        wo_part[:, f * cols : (f + 1) * cols] = value[f * size : (f + 1) * size]
    bias = jnp.broadcast_to(b_fc1[...], (size, b_fc1.shape[1]))
    units = chosen(where[0] * part, part, b_fc1.shape[1])
    wo_part[:, folds * cols : folds * cols + part] = dot(bias, units, NT).astype(BF16)


def pack_body(part, where, w_fc1, w_fc2, first, second):
    units = chosen(where[0] * part, part, w_fc2.shape[0])
    first[...] = dot(units, w_fc1[...], NT).astype(BF16)
    if part % 16 == 0:
        second[...] = w_fc2[pl.ds(pl.multiple_of(where[0] * part, 16), part), :]
    else:
        second[...] = dot(units, w_fc2[...], NN).astype(BF16)


def lay_body(folds, part, *refs):
    given, (out, biases) = refs[:-2], refs[-2:]
    size, count = given[0].shape[0], len(given)
    cols = out.shape[1] // count
    for s, ref in enumerate(given):
        at = (count - s) % count * cols
        for f in range(folds):
            out[f * size : (f + 1) * size, at : at + cols] = ref[:, f * cols : (f + 1) * cols]
        biases[s] = ref[:1, folds * cols : folds * cols + part].astype(F32)


def column(row):
    size = row.shape[1]
    same = lax.broadcasted_iota(jnp.int32, (size, size), 0) == lax.broadcasted_iota(jnp.int32, (size, size), 1)
    return jnp.sum(jnp.where(same, row, 0.0), axis=1, keepdims=True)


def load_body(cotangent, modulation, keep, logit, chan, payload, router):
    rows = cotangent.shape[0]
    routed = column(keep[...] * jax.nn.sigmoid(logit[...]))
    router[...] = routed
    payload[:rows] = (cotangent[...].astype(F32) * modulation[0, 5:6] * routed).astype(BF16)
    payload[rows:] = jnp.zeros((16, payload.shape[1]), BF16)
    payload[rows:, : chan.shape[1]] = jnp.broadcast_to(chan[...], (16, chan.shape[1])).astype(BF16)


def stack_body(*refs):
    begin = 0
    for ref in refs[:-1]:
        refs[-1][begin : begin + ref.shape[0]] = ref[...]
        begin += ref.shape[0]


def rows_of(refs, begin, end):
    found, at = [], 0
    for ref in refs:
        size = ref.shape[0]
        low, high = max(begin - at, 0), min(end - at, size)
        if low < high:
            found.append(ref[low:high])
        at += size
    return jnp.concatenate(found, axis=0) if len(found) > 1 else found[0]


def blocks_of(refs, rows):
    own, from_x, from_y, upper, lower, core = refs
    evens = [[own], [from_x], [from_y], [upper, lower]]
    return [b for i in range(4) for b in (evens[i], [core.at[i * rows : (i + 1) * rows]])]


def flags_body(part, per_quarter, quarters, order, first_group, *refs):
    masks = refs[-1]
    blocks = blocks_of(refs[:-1], refs[0].shape[0])
    units = masks.shape[1]
    quarter = lax.broadcasted_iota(jnp.int32, (1, units), 1) // part
    group = jnp.zeros((1, units), jnp.int32)
    for q in range(quarters):
        group = jnp.where(quarter == q, order[q] * per_quarter + first_group[0], group)
    groups = quarters * per_quarter
    spread = (lax.broadcasted_iota(jnp.int32, (groups, units), 0) == group).astype(BF16)
    end = refs[0].shape[0]
    for m, block in enumerate(blocks):
        chan = rows_of(block, end - 16, end)[:, :groups]
        masks[m : m + 1, :] = dot(chan, spread, NN)[:1]


def place_body(where, *refs):
    weights = refs[-1]
    quarters, width, cols = weights.shape
    out_cols = refs[0].shape[0]
    for m, block in enumerate(blocks_of(refs[:-1], out_cols)):
        at = pl.multiple_of(where[m] * out_cols, 16)
        rows = rows_of(block, 0, out_cols)
        for i in range(quarters):
            weights[i, pl.ds(at, out_cols), :] = rows[:, i * cols : (i + 1) * cols]


def head_of(refs, i):
    return join([r.at[:, i * LANES : i * LANES + HD] for r in refs])


def attend_body(rows, heads, order, segs, head_on, *refs):
    blocks = len(refs) - 1
    qkv, out = refs[:blocks], refs[blocks]
    cols = heads * HD
    scale = HD**-0.5 * LOG2E
    bias = jnp.concatenate(
        [jnp.full((1, rows), jnp.where(segs[j] == segs[order], 0.0, -1e30), F32) for j in range(blocks)], axis=1
    )
    folds = out.shape[1] // cols
    fold_rows = rows // folds
    for h in range(heads):
        q = head_of([qkv[order]], h)
        k = head_of(qkv, heads + h)
        v = head_of(qkv, 2 * heads + h)
        scores = dot(q, k, NT) * scale + bias
        powered = jnp.exp2(scores - jnp.max(scores, axis=1, keepdims=True))
        total = jnp.sum(powered, axis=1, keepdims=True)
        mixed = dot(powered.astype(BF16), v, NN) * (head_on[order, h] / total)
        mixed = mixed.astype(BF16)
        for f in range(folds):
            out[:, f * cols + h * HD : f * cols + (h + 1) * HD] = mixed[f * fold_rows : (f + 1) * fold_rows]


def unfold(ref, cols):
    folds = ref.shape[1] // cols
    return jnp.concatenate([ref[:, f * cols : (f + 1) * cols] for f in range(folds)], axis=0)


def project_body(cols, tokens, modulation, weight, *refs):
    pieces, (attn_out, middle, input_m) = refs[:-3], refs[-3:]
    rows = modulation[0]
    total = 0.0
    for s, piece in enumerate(pieces):
        total = total + dot(unfold(piece, cols), weight[s], NT)
    attn_out[...] = total
    value = tokens[...].astype(F32) + rows[2:3] * total
    middle[...] = value
    normed, _ = normalize(value)
    input_m[...] = (normed * (1.0 + rows[4:5]) + rows[3:4]).astype(BF16)


def join(refs):
    return jnp.concatenate([r[...] for r in refs], axis=0) if len(refs) > 1 else refs[0][...]


def mlp_body(sizes, quarters, part, picks, masks, bias, *refs):
    w1, w2 = join(refs[:quarters]), join(refs[quarters : 2 * quarters])
    refs = refs[2 * quarters :]
    count = sum(sizes)
    xs, refs = refs[:count], refs[count:]
    outs = refs[-2 - len(sizes) : -2]
    hidden_ref, grad_ref = refs[-2:]
    rows = outs[0].shape[0]
    givens = refs[: -2 - len(sizes)]
    givens = [[g] for g in givens] if len(givens) == 1 else blocks_of(givens, givens[0].shape[0])
    bias = jnp.concatenate([bias[q] for q in range(quarters)], axis=1)
    begin = 0
    for b, size in enumerate(sizes):
        x, g = join(xs[begin : begin + size]), rows_of(givens[picks[b]], 0, rows)
        begin += size
        mask = masks[picks[b] : picks[b] + 1, :]
        v = dot(x, w1, NT) + bias
        grad_hidden = dot(g, w2, NT)
        square = v * v
        t = jnp.tanh(GELU_ROOT * v * (1.0 + GELU_CUBE * square))
        half = 0.5 * (1.0 + t)
        slope = half + 0.5 * v * (1.0 - t * t) * (GELU_ROOT * (1.0 + 3.0 * GELU_CUBE * square))
        hidden_ref[b * rows : (b + 1) * rows, :] = (v * half * mask).astype(BF16)
        grad_pre = (grad_hidden * mask * slope).astype(BF16)
        grad_ref[b * rows : (b + 1) * rows, :] = grad_pre
        outs[b][...] = dot(grad_pre, w1, NN).astype(BF16)


def branch_body(quarters, count, *refs):
    w2, refs = join(refs[:quarters]), refs[quarters:]
    hiddens, (keep, send) = refs[:count], refs[count:]
    rows = keep.shape[1]
    b = 0
    for hidden in hiddens:
        for i in range(hidden.shape[0] // rows):
            (send if b % 2 else keep)[b // 2] = dot(hidden[i * rows : (i + 1) * rows, :], w2, NN).astype(BF16)
            b += 1


def split_rows(where, total, keep, send):
    size = keep.shape[1]
    for m in range(2 * keep.shape[0]):
        at = pl.multiple_of(where[m] * size, 16)
        (send if m % 2 else keep)[m // 2] = total[pl.ds(at, size), :].astype(BF16)


def fold_body(cut, count, whole, *refs):
    outs = list(refs[2 * count :])
    for i in range(count):
        total = (refs[i][...].astype(F32) + refs[count + i][...].astype(F32)).astype(BF16)
        if i < whole:
            outs.pop(0)[...] = total
        else:
            outs.pop(0)[...] = total[:cut]
            outs.pop(0)[...] = total[cut:]


def fc_grad_body(count, split, rows, order, *refs):
    acts, given, out, sums = refs[:count], refs[count:-2], refs[-2], refs[-1]
    if split:
        blocks = [rows_of(b, 0, rows) for b in blocks_of(given, given[0].shape[0])]
    else:
        blocks = [ref[...] for ref in given]
    given = jnp.concatenate(blocks, axis=0)
    acc, total, begin = 0.0, 0.0, 0
    for act in acts:
        size = act.shape[0]
        acc = acc + dot(act[...], given[begin : begin + size], TN)
        total = total + jnp.sum(act[...].astype(F32), axis=0, keepdims=True)
        begin += size
    sums[...] = total
    quarters = order.shape[0]
    part = out.shape[0] // quarters
    for s in range(quarters):
        out[pl.ds(pl.multiple_of(order[s] * part, 16), part), :] = acc[s * part : (s + 1) * part].astype(BF16)


def fc_turn_body(first, second, out):
    part, size = first.shape[0], out.shape[1]
    for i, total in enumerate((first, second)):
        for d in range(out.shape[0]):
            out[d, :, i * part : (i + 1) * part] = total[:, d * size : (d + 1) * size].T


def fc_leave_body(given, first, second):
    part = given.shape[2] // 2
    for d in range(given.shape[0]):
        first[:, d * part : (d + 1) * part] = given[d, :, :part].astype(F32)
        second[:, d * part : (d + 1) * part] = given[d, :, part:].astype(F32)


def total_of(begins, takes, refs):
    whole = refs[0][...].astype(F32)
    rows = whole.shape[0]
    for begin, take, ref in zip(begins[1:], takes[1:], refs[1:]):
        take = ref.shape[0] if take is None else take
        piece = ref[:take].astype(F32)
        if take < rows:
            blank = [jnp.zeros((n, piece.shape[1]), F32) for n in (begin, rows - begin - take)]
            piece = jnp.concatenate([b for b in (blank[0], piece, blank[1]) if b.shape[0]], axis=0)
        whole = whole + piece
    return whole


def middle_back_body(cols, begins, cotangent, modulation, middle, attn_out, weight, *refs):
    count = len(begins)
    grad_middle, grad_attn, sums = refs[count : count + 3]
    pieces = refs[count + 3 :]
    grad_in = total_of(begins, [None] * count, refs[:count])
    rows = modulation[0]
    normed, inv_std = normalize(middle[...])
    grad = cotangent[...].astype(F32) + norm_back(normed, inv_std, grad_in * (1.0 + rows[4:5]))
    grad_middle[...] = grad
    sums[0:1] = jnp.sum(grad * attn_out[...], axis=0, keepdims=True)
    sums[1:2] = jnp.sum(grad_in, axis=0, keepdims=True)
    sums[2:3] = jnp.sum(grad_in * normed, axis=0, keepdims=True)
    low = (grad * rows[2:3]).astype(BF16)
    grad_attn[...] = low
    folds = pieces[0].shape[1] // cols
    fold_rows = low.shape[0] // folds
    for s, piece in enumerate(pieces):
        value = dot(low, weight[s], NN).astype(BF16)
        for f in range(folds):
            piece[:, f * cols : (f + 1) * cols] = value[f * fold_rows : (f + 1) * fold_rows]


def attend_back_body(rows, heads, segs, head_on, *refs):
    blocks = (len(refs) - 2) // 3
    qkv, grads, outs = refs[:blocks], refs[blocks : 2 * blocks], refs[2 * blocks : 3 * blocks]
    dk_ref, dv_ref = refs[3 * blocks :]
    cols = heads * HD
    scale = HD**-0.5 * LOG2E
    given = [unfold(g, cols) for g in grads]
    for i in range(blocks):
        bias = jnp.concatenate(
            [jnp.full((rows, 1), jnp.where(segs[j] == segs[i], 0.0, -1e30), F32) for j in range(blocks)], axis=0
        )
        for h in range(heads):
            q = head_of([qkv[i]], h)
            k = head_of(qkv, heads + h)
            v = head_of(qkv, 2 * heads + h)
            g = (given[i][:, h * HD : (h + 1) * HD].astype(F32) * head_on[i, h]).astype(BF16)
            scores = dot(k, q, NT) * scale + bias
            powered = jnp.exp2(scores - jnp.max(scores, axis=0, keepdims=True))
            prob = powered * (1.0 / jnp.sum(powered, axis=0, keepdims=True))
            grad_prob = dot(v, g, NT)
            inner = jnp.sum(prob * grad_prob, axis=0, keepdims=True)
            grad_score = (prob * (grad_prob - inner)).astype(BF16)
            dv = dot(prob.astype(BF16), g, NN)
            dk = dot(grad_score, q, NN)
            dq = dot(grad_score, k, TN)
            outs[i][:, h * HD : (h + 1) * HD] = (dq * HD**-0.5).astype(BF16)
            dk_ref[h] = dk if i == 0 else dk_ref[h] + dk
            dv_ref[h] = dv if i == 0 else dv_ref[h] + dv
    for h in range(heads):
        for i in range(blocks):
            dk = dk_ref[h, i * rows : (i + 1) * rows, :] * HD**-0.5
            dv = dv_ref[h, i * rows : (i + 1) * rows, :]
            outs[i][:, cols + h * HD : cols + (h + 1) * HD] = dk.astype(BF16)
            outs[i][:, 2 * cols + h * HD : 2 * cols + (h + 1) * HD] = dv.astype(BF16)


def qkv_grads_body(blocks, *refs):
    xs, gs = refs[:blocks], refs[blocks : 2 * blocks]
    acc = 0.0
    for x, g in zip(xs, gs):
        acc = acc + dot(x[...], g[...], TN)
    refs[-1][...] = acc.astype(BF16)


def out_grads_body(cols, blocks, where, grad, *refs):
    outs, total = refs[blocks:-1], refs[-1]
    for s, piece in enumerate(refs[:blocks]):
        total[:, s * cols : (s + 1) * cols] = dot(grad[...], unfold(piece, cols), TN)
    if len(outs) == 1:
        outs[0][...] = total[...].astype(BF16)
        return
    split_rows(where, total, *outs)


def fold_b_body(cut, x, x_got, y, y_got, via_x, via_y, x_upper, y_lower, last_x, last_y):
    for_x = x[...].astype(F32) + x_got[...].astype(F32)
    for_y = y[...].astype(F32) + y_got[...].astype(F32)
    x_upper[...] = for_x[:cut].astype(BF16)
    last_x[...] = (for_x[cut:] + via_y[...].astype(F32)).astype(BF16)
    last_y[...] = (for_y[:cut] + via_x[...].astype(F32)).astype(BF16)
    y_lower[...] = for_y[cut:].astype(BF16)


def fold_near_body(cut, keep, got, own, for_x, for_y, send_x, send_y):
    rows = own.shape[0]
    blocks = [(keep[i].astype(F32) + got[i].astype(F32)).astype(BF16) for i in range(4)]
    own[...] = blocks[0]
    for_x[...] = blocks[1][cut:]
    for_y[...] = blocks[2][:cut]
    send_x[:cut] = blocks[1][:cut]
    send_x[cut:] = blocks[3][:cut]
    send_y[: rows - cut] = blocks[2][cut:]
    send_y[rows - cut :] = blocks[3][cut:]


def add_body(*refs):
    count = len(refs) // 3
    for a, b, out in zip(refs[:count], refs[count : 2 * count], refs[2 * count :]):
        out[...] = (a[...].astype(F32) + b[...].astype(F32)).astype(BF16)


def far_body(count, *refs):
    for i in range(count):
        for_x, for_y, got_x, got_y = refs[4 * i : 4 * i + 4]
        last_x, last_y = refs[4 * count + 2 * i : 4 * count + 2 * i + 2]
        cut, rest = for_y.shape[0], for_x.shape[0]
        last_x[...] = (for_x[...].astype(F32) + got_y[rest:].astype(F32)).astype(BF16)
        last_y[...] = (for_y[...].astype(F32) + got_x[cut:].astype(F32)).astype(BF16)


def parts_body(count, weight, *refs):
    for g, out in zip(refs[:count], refs[count:]):
        out[...] = dot(g[...], weight[...], NT).astype(BF16)


def out_sum_body(begins, takes, *refs):
    total = total_of(begins, takes, refs[: len(begins)])
    pieces = refs[len(begins) :]
    cols = pieces[0].shape[1]
    for s, piece in enumerate(pieces):
        piece[...] = total[:, s * cols : (s + 1) * cols].astype(BF16)


def qkv_leave_body(given, out):
    cols = out.shape[2]
    for i in range(3):
        out[:, i, :] = given[:, i * cols : (i + 1) * cols].astype(F32)


def leave_body(begins, takes, cotangent, router, modulation, middle, *refs):
    count = len(begins)
    output, sums = refs[count:]
    routed = router[...] * total_of(begins, takes, refs[:count])
    output[...] = (middle[...] + modulation[0, 5:6] * routed).astype(BF16)
    sums[...] = jnp.sum(cotangent[...].astype(F32) * routed, axis=0, keepdims=True)


def null_body(flags, *refs):
    count = (len(refs) - 1) // 2
    xs, parts, out = refs[:count], refs[count : 2 * count], refs[-1]
    first, second = 0.0, 0.0
    for s in range(count):
        normed, _ = normalize(xs[s][...].astype(F32))
        grad = parts[s][...].astype(F32) * flags[s]
        first = first + jnp.sum(grad, axis=0, keepdims=True)
        second = second + jnp.sum(grad * normed, axis=0, keepdims=True)
    out[0:1] = first
    out[1:2] = second


def token_back_body(tokens, modulation, grad_middle, own, received, grad_tokens):
    normed, inv_std = normalize(tokens[...].astype(F32))
    grad_in = own[...].astype(F32) + received[...].astype(F32)
    grad = grad_middle[...] + norm_back(normed, inv_std, grad_in * (1.0 + modulation[0, 1:2]))
    grad_tokens[...] = grad.astype(BF16)


def after(value, *others):
    return lax.optimization_barrier((value, others))[0]


def together(*values):
    return lax.optimization_barrier(values)


def shift(value, axis, size, step):
    return lax.ppermute(value, axis, [(i, (i + step) % size) for i in range(size)])


def swap(value, axis, size, bit):
    return lax.ppermute(value, axis, [(i, i ^ bit) for i in range(size)])


def ring_gather(block, axis, size):
    blocks = [block]
    for _ in range(size - 1):
        blocks.append(shift(blocks[-1], axis, size, 1))
    return blocks


def ring_reduce(parts, axis, size):
    total = parts[1 % size]
    for step in range(2, size + 1):
        total = shift(total, axis, size, 1)
        if step < size:
            total = total + parts[step]
    return parts[0], total


def cube_gather(block, axis, size):
    block = block[None]
    bit = 1
    while bit < size:
        block = jnp.concatenate([block, swap(block, axis, size, bit)], axis=0)
        bit *= 2
    return block


def cube_sum(value, axis, size):
    bit = 1
    while bit < size:
        value = value + swap(value, axis, size, bit)
        bit *= 2
    return value


def shift_all(parts, axis, size, sign):
    return [parts[0]] + [shift(parts[s], axis, size, sign * s) for s in range(1, size)]


def far(from_x, from_y, cut):
    return [swap(from_y[:cut], "dp", 8, 2), swap(from_x[cut:], "dp", 8, 4)]


def with_core(name, blocks):
    rows = sum(b.shape[0] for b in blocks)
    stacked = call(stack_body, name, shaped((rows, blocks[0].shape[1]), BF16), [], blocks)
    return [*blocks, swap(stacked, "dp", 8, 1)]


def add(name, *pairs):
    return call(
        add_body, name, tuple(shaped(a.shape, BF16) for a, _ in pairs), [], [a for a, _ in pairs] + [b for _, b in pairs]
    )


def fold(name, pairs, cut):
    rows, cols = pairs[0][0].shape
    return call(
        functools.partial(fold_body, cut, len(pairs), 0),
        name,
        tuple([shaped((cut, cols), BF16), shaped((rows - cut, cols), BF16)] * len(pairs)),
        [],
        [a for a, _ in pairs] + [b for _, b in pairs],
    )


def reduce_near(name, keep, got, cut):
    _, rows, cols = keep.shape
    sizes = (rows, rows - cut, cut, 2 * cut, 2 * (rows - cut))
    own, for_x, for_y, send_x, send_y = call(
        functools.partial(fold_near_body, cut),
        name,
        tuple(shaped((n, cols), BF16) for n in sizes),
        [],
        [keep, got],
    )
    return [own, for_x, for_y, swap(send_x, "dp", 8, 2), swap(send_y, "dp", 8, 4)]


def reduce_far(name, *states):
    shapes = [shaped(a.shape, BF16) for state in states for a in state[1:3]]
    marks = call(functools.partial(far_body, len(states)), name, tuple(shapes), [], [a for st in states for a in st[1:]])
    found = []
    for i, (own, for_x, for_y, got_x, got_y) in enumerate(states):
        cut, rest = for_y.shape[0], for_x.shape[0]
        last_x, last_y = swap(marks[2 * i], "dp", 8, 2), swap(marks[2 * i + 1], "dp", 8, 4)
        found.append(([0, 0, cut, 0, cut], [None, cut, None, None, rest], [own, got_x, last_x, last_y, got_y]))
    return *found, marks


def local(
    tokens,
    w_qkv,
    w_out,
    w_fc1,
    b_fc1,
    w_fc2,
    null_embed,
    ada_embed,
    item_len,
    null_flag,
    head_mask,
    group_mask,
    token_keep,
    router_logit,
    cotangent,
):
    n_tensor = lax.axis_size("tensor")
    n_dp = lax.axis_size("dp")
    z = lax.axis_index("tensor")
    p = lax.axis_index("dp")
    rows, width = tokens.shape
    group_rows = rows * n_tensor
    local_cols = w_qkv.shape[2]
    local_heads = local_cols // HD
    local_hidden = w_fc1.shape[1]
    part = local_hidden // n_dp
    hidden_units = part * n_tensor
    out_cols = width // n_dp
    slots = item_len.shape[1]
    chan_size = local_hidden * n_tensor // group_mask.shape[2]
    local_groups = group_mask.shape[2] // n_tensor
    folds = 4
    assert SHORT % rows == 0 and chan_size % part == 0 and n_dp & (n_dp - 1) == 0
    piece_shape = shaped((rows // folds, folds * local_cols), BF16)
    block_shape = shaped((rows, width), BF16)

    cube = n_dp == 8 and n_tensor == 4
    payload_rows = rows + 16
    cut = payload_rows // 2 // 16 * 16
    half = rows // 2
    out_cut = out_cols // 2 // 16 * 16
    lengths, flags = item_len[0], null_flag[0]

    rows_x = [tokens, shift(tokens, "tensor", n_tensor, 1)]
    mine_index = p[None].astype(jnp.int32)
    peers = (p ^ jnp.arange(n_dp)).astype(jnp.int32)
    order = ((z - jnp.arange(n_tensor)) % n_tensor).astype(jnp.int32)
    first_group = (p * part // chan_size)[None].astype(jnp.int32)
    wo_folds = 3 if out_cols % 48 == 0 else 1
    wo_lanes = -(-(wo_folds * local_cols + part) // LANES) * LANES
    wo_part = call(
        functools.partial(prepare_body, part, wo_folds),
        "prepare",
        shaped((out_cols // wo_folds, wo_lanes), BF16),
        [mine_index],
        [b_fc1[None], w_out],
    )
    wo_mine = [wo_part, shift(wo_part, "tensor", n_tensor, 1)]

    starts = order * rows
    ends = jnp.sum(jnp.where(jnp.arange(slots)[:, None] >= jnp.arange(slots)[None, :], lengths[None, :], 0), axis=1)
    segments = jnp.sum((ends[None, :] <= starts[:, None]).astype(jnp.int32), axis=1)
    hot = (segments[:, None] == jnp.arange(slots)[None, :]).astype(F32)
    heads_here = lax.dynamic_slice_in_dim(head_mask[0], z * local_heads, local_heads, 1).astype(F32)
    head_on = jnp.sum(hot[:, :, None] * heads_here[None], axis=1)
    nulls = jnp.sum(hot * flags.astype(F32)[None], axis=1)
    my_chan = jnp.sum(hot[0][:, None] * group_mask[0].astype(F32), axis=0)[None]
    modulation = call(
        items_body,
        "items",
        shaped((n_tensor, 6, width), F32),
        [segments, flags],
        [null_embed, ada_embed[0]],
    )
    payload, router = call(
        load_body,
        "load",
        (shaped((payload_rows, width), BF16), shaped((rows, 1), F32)),
        [],
        [cotangent, modulation, token_keep.astype(F32)[None], router_logit[None], my_chan],
    )
    flat_qkv = w_qkv.reshape(width, 3 * local_cols)

    def project_in(s, block):
        return call(
            functools.partial(qkv_body, s),
            f"qkv_{s}",
            (block_shape, shaped((rows, 3 * local_heads * LANES), BF16)),
            [],
            [block, modulation, flat_qkv],
        )

    rows_x[1], wo_mine[1], payload = together(rows_x[1], wo_mine[1], payload)
    if cube:
        pay_x, pay_y = swap(payload, "dp", n_dp, 2), swap(payload, "dp", n_dp, 4)
    rows_x.append(shift(rows_x[1], "tensor", n_tensor, 1))
    wo_mine.append(shift(wo_mine[1], "tensor", n_tensor, 1))
    w1_part, w2_part = call(
        functools.partial(pack_body, part),
        "pack",
        (shaped((part, width), BF16),) * 2,
        [after(mine_index, payload)],
        [w_fc1, w_fc2],
    )
    input_a, qkv = zip(project_in(0, after(rows_x[0], rows_x[1])), project_in(1, rows_x[1]))
    input_a, qkv = [*input_a], [*qkv]
    rows_x[2], wo_mine[2], w1_part, qkv = together(rows_x[2], wo_mine[2], w1_part, qkv)
    for s in range(2, n_tensor):
        if s + 1 < n_tensor:
            rows_x.append(shift(rows_x[s], "tensor", n_tensor, 1))
            wo_mine.append(shift(wo_mine[s], "tensor", n_tensor, 1))
        if cube and s == 2:
            pay_x, pay_y = after((pay_x, pay_y), rows_x[2])
            pay_far = far(pay_x, pay_y, cut)
        low, value = project_in(s, rows_x[s])
        input_a.append(low)
        qkv.append(value)
        if cube and s == 2:
            pay_blocks = [payload, pay_x, pay_y, *pay_far]
            pay_stack = call(
                stack_body, "stack_pay", shaped((4 * payload_rows, width), BF16), [], after(pay_blocks, value)
            )
            rows_x[3], wo_mine, value, pay_stack, w1_part = together(rows_x[3], wo_mine, value, pay_stack, w1_part)
            qkv[2] = value
        elif s + 1 < n_tensor:
            rows_x[s + 1] = after(rows_x[s + 1], value)
    w1 = [w1_part, shift(after(w1_part, rows_x[-1]), "tensor", n_tensor, 1)]
    wo_flat, biases = call(
        functools.partial(lay_body, wo_folds, part),
        "lay",
        (shaped((out_cols, n_tensor * local_cols), BF16), shaped((n_tensor, 1, part), F32)),
        [],
        wo_mine,
    )
    if cube:
        pay_core = swap(pay_stack, "dp", n_dp, 1)
        wo_x, wo_y = swap(wo_flat, "dp", n_dp, 2), swap(wo_flat, "dp", n_dp, 4)

    def attend(s, qkv):
        return call(
            functools.partial(attend_body, rows, local_heads, s),
            f"attend_{s}",
            piece_shape,
            [segments, head_on],
            [*qkv],
        )

    pieces, mine = {}, {}
    away = [n_tensor // 2] + [s for s in range(1, n_tensor) if s != n_tensor // 2]
    for step, s in enumerate([*away, 0]):
        pieces[s] = attend(s, qkv)
        qkv = after(qkv, pieces[s])
        if step == 1 and cube:
            pieces, w1[1], wo_x, wo_y, pay_core, qkv = together(pieces, w1[1], wo_x, wo_y, pay_core, qkv)
            w1.append(shift(w1[1], "tensor", n_tensor, 1))
            wo_far = far(wo_x, wo_y, out_cut)
    if cube:
        sent = {s: shift(pieces[s], "tensor", n_tensor, -s) for s in away[:2]}
        wo_blocks = [wo_flat, wo_x, wo_y, *wo_far]
        pieces, w1[2], wo_far, wo_stack = together(
            pieces, w1[2], wo_far, call(stack_body, "stack_wo", shaped((4 * out_cols, width), BF16), [], wo_blocks)
        )
        wo_core = swap(wo_stack, "dp", n_dp, 1)
        w1.append(shift(w1[2], "tensor", n_tensor, 1))
        wo_all = call(
            place_body,
            "place",
            shaped((n_tensor, width, local_cols), BF16),
            [peers],
            [wo_flat, wo_x, wo_y, *wo_far, wo_core],
        )
        payloads = [payload, pay_x, pay_y, *pay_far, pay_core]
        masks = call(
            functools.partial(flags_body, part, local_groups, n_tensor),
            "flags",
            shaped((n_dp, hidden_units), F32),
            [order, first_group],
            after(payloads, pieces[0]),
        )
        mine = [pieces[0] if s == 0 else sent[s] if s in sent else shift(pieces[s], "tensor", n_tensor, -s) for s in range(n_tensor)]
        mine, wo_all, masks = together(mine, wo_all, masks)
    else:
        mine = shift_all([pieces[s] for s in range(n_tensor)], "tensor", n_tensor, -1)
        wo_all = lax.all_gather(wo_flat, "dp", axis=0).reshape(n_dp, out_cols, n_tensor, local_cols)
        wo_all = wo_all.transpose(2, 0, 1, 3).reshape(n_tensor, width, local_cols)
        payloads = lax.all_gather(payload, "dp", axis=0)
        chan = payloads[:, rows, : n_tensor * local_groups].astype(F32)
        chan = chan.reshape(n_dp, n_tensor, local_groups)
        chan = lax.dynamic_index_in_dim(chan, first_group[0], 2, False)[:, order]
        masks = jnp.repeat(chan, part, axis=1)
        while len(w1) < n_tensor:
            w1.append(shift(w1[-1], "tensor", n_tensor, 1))
        w2 = ring_gather(w2_part, "tensor", n_tensor)
    attn_out, middle, input_m = call(
        functools.partial(project_body, local_cols),
        "project",
        (shaped((rows, width), F32), shaped((rows, width), F32), block_shape),
        [],
        [tokens, modulation, wo_all, *mine],
    )

    def mlp(name, picks, masks, xs, gs):
        acts = shaped((len(xs) * rows, hidden_units), BF16)
        return call(
            functools.partial(mlp_body, [len(x) for x in xs], n_tensor, part, picks),
            name,
            (*[block_shape] * len(xs), acts, acts),
            [],
            [masks, biases, *w1, *w2, *sum(xs, []), *gs],
        )

    def fc_grad(name, acts, arrays, split):
        return call(
            functools.partial(fc_grad_body, len(acts), split, rows),
            name,
            (shaped((hidden_units, width), BF16), shaped((1, hidden_units), F32)),
            [order],
            [*acts, *arrays],
        )

    if cube:
        core, from_x, from_y = [swap(input_m, "dp", n_dp, bit) for bit in (1, 2, 4)]
        w2 = [w2_part, shift(after(w2_part, w1[3]), "tensor", n_tensor, 1)]
        core, from_x, from_y, w2[1] = together(core, from_x, from_y, w2[1])
        w2.append(shift(w2[1], "tensor", n_tensor, 1))
        upper, lower = far(from_x, from_y, half)
        from_xc, from_yc = swap(from_x, "dp", n_dp, 1), swap(from_y, "dp", n_dp, 1)
        near_x, upper, lower, w2[2] = together([from_x, from_xc, from_y, from_yc], upper, lower, w2[2])
        w2.append(shift(w2[2], "tensor", n_tensor, 1))
        upper_c, lower_c = swap(upper, "dp", n_dp, 1), swap(lower, "dp", n_dp, 1)
        far_x = [upper, lower, upper_c, lower_c]
        w2[3], far_x = together(w2[3], far_x)
        *part_c, hidden_c, pre_c = mlp("mlp_6", (6, 7), masks, [far_x[:2], far_x[2:]], payloads)
        cross = fold("fold_c", [(part_c[0], swap(part_c[1], "dp", n_dp, 1))], half)
        near_x, cross = together(near_x, cross)
        via_x, via_y = swap(cross[0], "dp", n_dp, 2), swap(cross[1], "dp", n_dp, 4)
        *part_b, hidden_b, pre_b = mlp("mlp_2", (2, 3, 4, 5), masks, [[b] for b in near_x], payloads)
        part_b, via_x, via_y = together(part_b, via_x, via_y)
        part_b = [(part_b[m], swap(part_b[m + 1], "dp", n_dp, 1)) for m in (0, 2)]
        x_upper, y_lower, last_x, last_y = call(
            functools.partial(fold_b_body, half),
            "fold_b",
            (shaped((half, width), BF16),) * 4,
            [],
            [*part_b[0], *part_b[1], via_x, via_y],
        )
        first_x, x_upper, y_lower, last_x, last_y = together([input_m, core], x_upper, y_lower, last_x, last_y)
        x_upper, y_lower = swap(x_upper, "dp", n_dp, 2), swap(y_lower, "dp", n_dp, 4)
        x_lower, y_upper = swap(last_x, "dp", n_dp, 2), swap(last_y, "dp", n_dp, 4)
        *part_a, hidden_a, pre_a = mlp("mlp_0", (0, 1), masks, [[b] for b in first_x], payloads)
        hiddens, grad_pres = [hidden_a, hidden_b, hidden_c], [pre_a, pre_b, pre_c]
        rows_m = [*first_x, *near_x, *far_x]
        grad_fc2, _ = fc_grad("fc2_grad", hiddens, payloads, True)
        own = [part_a[0], swap(part_a[1], "dp", n_dp, 1)]
        branch_keep, branch_send = call(
            functools.partial(branch_body, n_tensor, len(hiddens)),
            "branch",
            tuple([shaped((n_dp // 2, rows, width), BF16)] * 2),
            [],
            [*w2, *after(hiddens, grad_fc2)],
        )
        grad_in_m = [*own, x_upper, x_lower, y_upper, y_lower]
        begins = [0, 0, 0, half, 0, half]
        grad_in_m, branch_keep, branch_send = together(grad_in_m, branch_keep, branch_send)
    else:
        rows_m = lax.all_gather(input_m, "dp", axis=0)

        def step(sums, given):
            x, g, m = given
            out, hidden, grad_pre = mlp("mlp", (0,), m[None], [[x]], [g])
            sums = [a + dot(b, c, TN) for a, b, c in zip(sums, (grad_pre, hidden), (x, g[:rows]))]
            return sums, (out, hidden, jnp.sum(grad_pre.astype(F32), axis=0, keepdims=True))

        zero = jnp.zeros((hidden_units, width), F32)
        sums, (grad_parts, hidden, grad_bias) = lax.scan(step, [zero, zero], (rows_m, payloads, masks))
        begins, grad_in_m = [0], [lax.psum_scatter(grad_parts, "dp", scatter_dimension=0)]
        grad_bias = jnp.sum(grad_bias, axis=0)
        sums = [a.astype(BF16).reshape(n_tensor, part, width) for a in sums]
        grad_fc1, grad_fc2 = [jnp.take(a, order, axis=0).reshape(hidden_units, width) for a in sums]

    def fc_scatter(value):
        return lax.psum_scatter(value.reshape(n_tensor, part, width), "tensor", scatter_dimension=0)

    fc2_sum = fc_scatter(grad_fc2)
    grad_middle, grad_attn, sums_m, *grad_pieces = call(
        functools.partial(middle_back_body, local_cols, begins),
        "middle_back",
        (shaped((rows, width), F32), block_shape, shaped((3, width), F32), *[piece_shape] * n_tensor),
        [],
        [cotangent, modulation, middle, attn_out, wo_all, *grad_in_m],
    )
    grads = shift_all(grad_pieces, "tensor", n_tensor, 1)
    late_attn = after(grad_attn, grad_pieces)

    if cube:
        grad_fc1, grad_bias = fc_grad("fc1_grad", after(grad_pres, late_attn), rows_m, False)
        late_attn = after(late_attn, grad_bias)
    grad_wout = call(
        functools.partial(out_grads_body, local_cols, n_tensor),
        "out_grads",
        (shaped((4, out_cols, width), BF16),) * 2 if cube else (shaped((width, width), BF16),),
        [peers],
        [late_attn, *mine],
        scratch=[pltpu.VMEM((width, width), F32)],
    )
    if cube:
        branch_got = swap(branch_send, "dp", n_dp, 1)
        grads, branch_got, grad_wout, grad_fc1 = together(grads, branch_got, grad_wout, grad_fc1)
        wout_got = swap(grad_wout[1], "dp", n_dp, 1)
        branch_state = reduce_near("branch_near", branch_keep, branch_got, half)
        grads = after(grads, branch_state[0])
    else:
        w2 = jnp.concatenate(w2, axis=0)
        branch = after(hidden, grad_fc1).reshape(n_dp * rows, hidden_units)
        branch = dot(branch, w2, NN).astype(BF16).reshape(n_dp, rows, width)
        late_begins, takes, branch = [0], [None], [lax.psum_scatter(branch, "dp", scatter_dimension=0)]
        wout_sum = lax.psum_scatter(grad_wout[0].reshape(n_dp, out_cols, width), "dp", scatter_dimension=0)
    fc1_sum = fc_scatter(grad_fc1)

    grad_rows = call(
        functools.partial(attend_back_body, rows, local_heads),
        "attend_back",
        tuple([shaped((rows, 3 * local_cols), BF16)] * n_tensor),
        [segments, head_on],
        [*qkv, *grads],
        scratch=[pltpu.VMEM((local_heads, group_rows, HD), F32)] * 2,
        limit=48,
    )

    def grad_parts_of(name, given):
        return call(
            functools.partial(parts_body, len(given)), name, (block_shape,) * len(given), [], [flat_qkv, *given]
        )

    (first,) = grad_parts_of("part_1", [grad_rows[1]])
    later = after(grad_rows, first)
    if cube:
        first, later, branch_state, wout_got = together(first, later, branch_state, wout_got)
    total = shift(first, "tensor", n_tensor, 1)
    grad_wqkv = call(
        functools.partial(qkv_grads_body, n_tensor),
        "qkv_grads",
        shaped((width, 3 * local_cols), BF16),
        [],
        [*input_a, *later],
    )
    qkv_sum = lax.psum_scatter(grad_wqkv.reshape(n_dp, out_cols, 3 * local_cols), "dp", scatter_dimension=0)
    later = after(later, grad_wqkv)
    if cube:
        (late_begins, takes, branch), branch_marks = reduce_far("branch_far", after(branch_state, grad_wqkv))
        wout_state = reduce_near("wout_near", *after((grad_wout[0], wout_got), branch_marks), out_cut)
        later = after(later, wout_state[0])
    others = [s for s in range(n_tensor) if s != 1]
    grad_in_parts = dict(zip(others, grad_parts_of("parts", [later[s] for s in others])))
    grad_in_parts = [first if s == 1 else grad_in_parts[s] for s in range(n_tensor)]
    sums_a = call(null_body, "null", shaped((2, width), F32), [nulls], [*rows_x, *grad_in_parts])
    if cube:
        total, grad_in_parts, branch, wout_state, sums_a = together(total, grad_in_parts, branch, wout_state, sums_a)
    total = total + grad_in_parts[2 % n_tensor]
    mark = total
    total = shift(total, "tensor", n_tensor, 1)
    if cube:
        (wout_begins, wout_takes, wout_last), wout_marks = reduce_far("wout_far", after(wout_state, mark))
        branch = after(branch, wout_marks)
    output, sums_b = call(
        functools.partial(leave_body, late_begins, takes),
        "leave",
        (block_shape, shaped((1, width), F32)),
        [],
        [cotangent, router, modulation, middle, *branch],
    )
    bias_full = lax.dynamic_update_slice_in_dim(
        jnp.zeros((n_tensor, local_hidden), F32), grad_bias.reshape(n_tensor, part)[order], p * part, 1
    )
    small = jnp.concatenate(
        [bias_full.reshape(-1, width), sums_a, nulls[0] * sums_m, nulls[0] * sums_b], axis=0
    )
    small = cube_sum(small, "dp", n_dp)
    if cube:
        total, small, wout_last = together(total, small, wout_last)
    for s in range(3, n_tensor):
        total = total + grad_in_parts[s]
        mark = total
        total = shift(total, "tensor", n_tensor, 1)

    small = small + swap(small, "tensor", n_tensor, 1)
    mark = small
    bit = 2
    while bit < n_tensor:
        small = small + swap(small, "tensor", n_tensor, bit)
        bit *= 2
    if cube:
        wout_parts = call(
            functools.partial(out_sum_body, wout_begins, wout_takes),
            "out_sum",
            tuple([shaped((out_cols, local_cols), BF16)] * n_tensor),
            [],
            wout_last,
        )
    else:
        wout_parts = [wout_sum[:, i * local_cols : (i + 1) * local_cols] for i in range(n_tensor)]
    wout_parts = shift_all(wout_parts, "tensor", n_tensor, 1)
    fc_sum = call(
        fc_turn_body,
        "fc_turn",
        shaped((n_dp, out_cols, 2 * part), BF16),
        [],
        after([fc1_sum, fc2_sum], mark),
    )
    fc_sum = lax.all_to_all(fc_sum, "dp", split_axis=0, concat_axis=0)
    qkv_sum = call(
        qkv_leave_body,
        "qkv_leave",
        shaped((out_cols, 3, local_cols), F32),
        [],
        [qkv_sum],
    )
    fc1_sum, fc2_sum = call(
        fc_leave_body,
        "fc_leave",
        (shaped((out_cols, local_hidden), F32), shaped((out_cols, local_hidden), F32)),
        [],
        [fc_sum],
    )
    wout_sum = sum(x.astype(F32) for x in wout_parts).T
    bias_sum, null_sum = small[:-6].reshape(-1), small[-6:]
    grad_tokens = call(
        token_back_body,
        "token_back",
        block_shape,
        [],
        [tokens, modulation, grad_middle, grad_in_parts[0], total],
    )

    return (
        output,
        grad_tokens,
        qkv_sum,
        wout_sum,
        fc1_sum,
        bias_sum,
        fc2_sum.T,
        null_sum,
    )


def solution(mesh):
    in_specs = (
        P(("dp", "tensor"), None),
        P(None, None, "tensor"),
        P("tensor", None),
        P(None, "tensor"),
        P("tensor"),
        P("tensor", None),
        P(),
        P("dp", None, None, None),
        P("dp", None),
        P("dp", None),
        P("dp", None, None),
        P("dp", None, None),
        P(("dp", "tensor")),
        P(("dp", "tensor")),
        P(("dp", "tensor"), None),
    )
    out_specs = (
        P(("dp", "tensor"), None),
        P(("dp", "tensor"), None),
        P("dp", None, "tensor"),
        P("tensor", "dp"),
        P("dp", "tensor"),
        P(),
        P("tensor", "dp"),
        P(),
    )
    return jax.shard_map(local, mesh=mesh, in_specs=in_specs, out_specs=out_specs, check_vma=False)
```
